128 devices in a mesh: seq: 64 (over y, z_lo, x, core), head: 2 (over z_hi).
Axes of the slice: x: 4, y: 4, z: 4 (z_hi: 2, z_lo: 2; z = z_hi * 2 + z_lo), core: 2. Of those that a mesh axis runs over, the one named last changes fastest.
Arguments:
- queries: bfloat16 [32768, 768], P('seq', 'head'), may hold values from -6 to 6
- keys: bfloat16 [32768, 768], P('seq', 'head'), may hold values from -6 to 6
- values: bfloat16 [32768, 768], P('seq', 'head'), may hold values from -6 to 6
- offsets: int32 [2, 12], replicated, may hold values from 0 to 63, as said below
- w_out: bfloat16 [768, 768], P('head'), may hold values from -0.21875 to 0.21875
- grad_mixed: bfloat16 [32768, 768], P('seq', 'head'), may hold values from -6 to 6
Outputs:
- mixed: bfloat16 [32768, 768], P('seq', 'head')
- grad_queries: bfloat16 [32768, 768], P('seq', 'head')
- grad_keys: bfloat16 [32768, 768], P('seq', 'head')
- grad_values: bfloat16 [32768, 768], P('seq', 'head')
- grad_w_out: float32 [768, 768], P('head')
The draws below stay inside these ranges and needn't reach their ends.
Inputs may be any that keep to these rules, and one draw needn't show every extreme that they name: `offsets`: row 0 holds each head's offset at level 1, below 4; row 1 its offset at level 2, below 64.
All inputs are finite; a program needn't handle non-finite values.
Results may differ from the reference program's by a relative error of at most 0.023.
Values may be sent and summed in bfloat16 or wider, within the bound.
A program may use at most 128 MiB of HBM per device.

```python
import jax
import jax.numpy as jnp
from jax import lax

D = 768
HEADS = 12
HD = 64
G_MID = 4
TOK_DEV = 512
TOKENS = 32768
N_SEQ = 64


def draw_queries(key, part):
    key = jax.random.fold_in(key, 11)
    result = jnp.clip(jax.random.normal(key, (TOKENS, D), jnp.float32), -5.0, 5.0)
    return result.astype(jnp.bfloat16)


def draw_keys(key, part):
    key = jax.random.fold_in(key, 13)
    result = jnp.clip(jax.random.normal(key, (TOKENS, D), jnp.float32), -5.0, 5.0)
    return result.astype(jnp.bfloat16)


def draw_values(key, part):
    key = jax.random.fold_in(key, 17)
    result = jnp.clip(jax.random.normal(key, (TOKENS, D), jnp.float32), -6.0, 6.0)
    return result.astype(jnp.bfloat16)


def draw_grad_mixed(key, part):
    key = jax.random.fold_in(key, 19)
    result = jnp.clip(jax.random.normal(key, (TOKENS, D), jnp.float32), -6.0, 6.0)
    return result.astype(jnp.bfloat16)


def draw_offsets(key, part):
    key = jax.random.fold_in(key, 5)
    first_key, second_key, third_key = jax.random.split(key, 3)
    middle_row = jax.random.permutation(first_key, HEADS) % G_MID
    ranking = jax.random.permutation(second_key, HEADS)
    random_row = jax.random.randint(third_key, (HEADS,), 0, N_SEQ)
    top_row = jnp.where(ranking == 0, N_SEQ - 1, jnp.where(ranking == 1, 0, random_row))
    return jnp.stack([middle_row, top_row]).astype(jnp.int32)


def block_scale(key, dims, cuts, least, top_value):
    loudness = 1.0
    for axis_at, blocks in cuts:
        draws = jax.random.uniform(jax.random.fold_in(jax.random.fold_in(key, 6), axis_at), (blocks,), jnp.float32, least / len(cuts), top_value / len(cuts))
        loudness = loudness * jnp.repeat(jnp.exp(draws), dims[axis_at] // blocks).reshape((-1,) + (1,) * (len(dims) - 1 - axis_at))
    return loudness


def bell_draw(own_key, dims, scale, limit, cuts=(), held_as=jnp.bfloat16):
    values = scale * jax.random.normal(own_key, dims, jnp.float32)
    if cuts:
        values = values * block_scale(own_key, dims, cuts, -0.22, 0.18)
    return jnp.clip(values, -limit, limit).astype(held_as)


def setup_inputs(seed: int = 0) -> dict:
    arg_keys = jax.random.split(jax.random.key(seed), 7)
    queries = draw_queries(jax.random.fold_in(arg_keys[6], 71), 0)
    keys = draw_keys(jax.random.fold_in(arg_keys[6], 71), 0)
    values = draw_values(jax.random.fold_in(arg_keys[6], 71), 0)
    offsets = draw_offsets(jax.random.fold_in(arg_keys[6], 71), 0)
    w_out = bell_draw(arg_keys[4], (D, D), D ** -0.5, 0.21875, ((0, 2),))
    grad_mixed = draw_grad_mixed(jax.random.fold_in(arg_keys[6], 71), 0)
    return {"queries": queries, "keys": keys, "values": values, "offsets": offsets, "w_out": w_out, "grad_mixed": grad_mixed}


def hit_table(stride, offset):
    return jnp.arange(stride, dtype=jnp.int32)[:, None] == offset[None, :]


def pick_rows(source, stride, offset):
    trailing = source.shape[2:]
    grouped = source.reshape((source.shape[0] // stride, stride) + source.shape[1:])
    hits = hit_table(stride, offset).reshape((1, stride, source.shape[1]) + (1,) * len(trailing))
    return jnp.sum(jnp.where(hits, grouped, jnp.zeros((), source.dtype)), axis=1)


def put_rows(source, stride, offset):
    trailing = source.shape[2:]
    hits = hit_table(stride, offset).reshape((1, stride, source.shape[1]) + (1,) * len(trailing))
    spread = jnp.where(hits, source[:, None], jnp.zeros((), source.dtype))
    return spread.reshape((source.shape[0] * stride,) + source.shape[1:])


def segments(source):
    return source.reshape((-1, TOK_DEV) + source.shape[1:])


def seg_scores(query_seg, key_seg):
    return jnp.einsum("qhd,khd->hqk", query_seg.astype(jnp.float32), key_seg.astype(jnp.float32)) * 0.125


def seg_lse(inputs):
    query_seg, key_seg = inputs
    scores = seg_scores(query_seg, key_seg)
    highest = jnp.max(scores, axis=-1, keepdims=True)
    return (highest[..., 0] + jnp.log(jnp.sum(jnp.exp(scores - highest), axis=-1))).T


def seg_out(inputs):
    query_seg, key_seg, value_seg, lse_seg = inputs
    weights_bf = jnp.exp(seg_scores(query_seg, key_seg) - lse_seg.T[:, :, None]).astype(jnp.bfloat16)
    weights_bf = lax.optimization_barrier(weights_bf)
    return jnp.einsum("hqk,khd->qhd", weights_bf.astype(jnp.float32), value_seg.astype(jnp.float32))


def seg_grads(inputs):
    query_seg, key_seg, value_seg, grad_seg, lse_seg, delta_seg = inputs
    exact_probs = jnp.exp(seg_scores(query_seg, key_seg) - lse_seg.T[:, :, None])
    weights_bf = lax.optimization_barrier(exact_probs.astype(jnp.bfloat16)).astype(jnp.float32)
    grad_wide = grad_seg.astype(jnp.float32)
    grad_value = jnp.einsum("hqk,qhd->khd", weights_bf, grad_wide)
    grad_prob = jnp.einsum("qhd,khd->hqk", grad_wide, value_seg.astype(jnp.float32))
    dscore = (0.125 * exact_probs * (grad_prob - delta_seg.T[:, :, None])).astype(jnp.bfloat16)
    dscore = lax.optimization_barrier(dscore).astype(jnp.float32)
    grad_query = jnp.einsum("hqk,khd->qhd", dscore, key_seg.astype(jnp.float32))
    grad_key = jnp.einsum("hqk,qhd->khd", dscore, query_seg.astype(jnp.float32))
    return grad_query, grad_key, grad_value


def reference(queries, keys, values, offsets, w_out, grad_mixed):
    query_cube = queries.reshape(TOKENS, HEADS, HD)
    key_cube = keys.reshape(TOKENS, HEADS, HD)
    value_cube = values.reshape(TOKENS, HEADS, HD)
    levels = [(1, jnp.zeros((HEADS,), jnp.int32)), (G_MID, offsets[0].astype(jnp.int32)), (N_SEQ, offsets[1].astype(jnp.int32))]
    placed = []
    for stride, offset in levels:
        query_seg = segments(pick_rows(query_cube, stride, offset))
        key_seg = segments(pick_rows(key_cube, stride, offset))
        lse_sel = lax.map(seg_lse, (query_seg, key_seg)).reshape(-1, HEADS)
        marked = put_rows(jnp.ones_like(lse_sel), stride, offset) > 0.5
        placed.append((put_rows(lse_sel, stride, offset), marked))
    first_lse = placed[0][0]
    highest = first_lse
    for level_lse, marked in placed[1:]:
        highest = jnp.maximum(highest, jnp.where(marked, level_lse, highest))
    summed = jnp.exp(first_lse - highest)
    for level_lse, marked in placed[1:]:
        summed = summed + jnp.where(marked, jnp.exp(jnp.where(marked, level_lse, highest) - highest), jnp.float32(0.0))
    lse_all = highest + jnp.log(summed)
    attended = jnp.zeros((TOKENS, HEADS, HD), jnp.float32)
    for stride, offset in levels:
        inputs = (segments(pick_rows(query_cube, stride, offset)), segments(pick_rows(key_cube, stride, offset)),
                  segments(pick_rows(value_cube, stride, offset)), segments(pick_rows(lse_all, stride, offset)))
        level_out = lax.map(seg_out, inputs).reshape(-1, HEADS, HD)
        attended = attended + put_rows(level_out, stride, offset)
    attended = attended.astype(jnp.bfloat16)
    flat_attended = attended.reshape(TOKENS, D)
    mixed = jnp.dot(flat_attended, w_out, preferred_element_type=jnp.float32).astype(jnp.bfloat16)
    grad_w_out = jnp.dot(flat_attended.T, grad_mixed, preferred_element_type=jnp.float32)
    grad_attended = jnp.dot(grad_mixed, w_out.T, preferred_element_type=jnp.float32).astype(jnp.bfloat16)
    grad_cube = grad_attended.reshape(TOKENS, HEADS, HD)
    delta_all = jnp.sum(grad_cube.astype(jnp.float32) * attended.astype(jnp.float32), axis=2)
    grad_q_sum = jnp.zeros((TOKENS, HEADS, HD), jnp.float32)
    grad_k_sum = jnp.zeros((TOKENS, HEADS, HD), jnp.float32)
    grad_v_sum = jnp.zeros((TOKENS, HEADS, HD), jnp.float32)
    for stride, offset in levels:
        inputs = (segments(pick_rows(query_cube, stride, offset)), segments(pick_rows(key_cube, stride, offset)),
                  segments(pick_rows(value_cube, stride, offset)), segments(pick_rows(grad_cube, stride, offset)),
                  segments(pick_rows(lse_all, stride, offset)), segments(pick_rows(delta_all, stride, offset)))
        grad_query, grad_key, grad_value = lax.map(seg_grads, inputs)
        grad_q_sum = grad_q_sum + put_rows(grad_query.reshape(-1, HEADS, HD), stride, offset)
        grad_k_sum = grad_k_sum + put_rows(grad_key.reshape(-1, HEADS, HD), stride, offset)
        grad_v_sum = grad_v_sum + put_rows(grad_value.reshape(-1, HEADS, HD), stride, offset)
    grad_queries = grad_q_sum.astype(jnp.bfloat16).reshape(TOKENS, D)
    grad_keys = grad_k_sum.astype(jnp.bfloat16).reshape(TOKENS, D)
    grad_values = grad_v_sum.astype(jnp.bfloat16).reshape(TOKENS, D)
    return (mixed, grad_queries, grad_keys, grad_values, grad_w_out)
```

```python
import math

import jax
import jax.numpy as jnp
from jax import lax
from jax.experimental import pallas as pl
from jax.experimental.pallas import tpu as pltpu
from jax.sharding import PartitionSpec as P

HD = 64
TOK = 512
CHIPS = 32
OWNERS = 24
SCALE = 0.125 * math.log2(math.e)
MESH = pl.DeviceIdType.MESH
F32 = jnp.float32
BF16 = jnp.bfloat16


def nn(a, b):
    return lax.dot_general(a, b, (((1,), (0,)), ((), ())), preferred_element_type=F32)


def nt(a, b):
    return lax.dot_general(a, b, (((1,), (1,)), ((), ())), preferred_element_type=F32)


def tn(a, b):
    return lax.dot_general(a, b, (((0,), (0,)), ((), ())), preferred_element_type=F32)


def iota(shape, dim):
    return lax.broadcasted_iota(jnp.int32, shape, dim)


def halves(x):
    hi = x.astype(BF16)
    return hi, (x - hi.astype(F32)).astype(BF16)


def thirds(x):
    hi = x.astype(BF16).astype(F32)
    mid = (x - hi).astype(BF16).astype(F32)
    return [hi, mid, x - hi - mid]


def cols(p):
    return pl.ds(pl.multiple_of(p * 128, 128), 128)


def kernel(
    off_ref, q_ref, k_ref, v_ref, w_ref, g_ref,
    mixed_ref, dq_ref, dk_ref, dv_ref, dw_ref,
    kv1, x2, goth, qt, kt, vt, k1t, q1t, q2, e1, e2, p0, p1, p2, o0, o1, o2, st0, st1, st2,
    at, an, gs, gt, mxs, mxr, wps, wpo, wmr, wrs, wrr, wfull,
    do2, de2, dx, dxs, dxm, dxb, xr, dq2, dqx, dk1, dks, dkm, dkc, dkr, dk0, dv0,
    ssem, rsem,
):
    s = lax.axis_index("seq")
    h = lax.axis_index("head")
    chip, core = s // 2, lax.rem(s, 2)
    r = lax.rem(s, 4)
    mate = s + 1 - 2 * core
    side = lax.rem(chip, 2)
    facing = s + 2 - 4 * side
    r_mate = r + 1 - 2 * core
    r_facing = r + 2 - 4 * side
    r_other = r_mate + 2 - 4 * side
    first = h * 6
    to_mate, to_facing, to_half = (mate, h), (facing, h), (s, 1 - h)

    def peer(c):
        return (2 * c + core, h)

    def copy(src, dst, n, device):
        return pltpu.make_async_remote_copy(
            src_ref=src, dst_ref=dst, send_sem=ssem.at[n], recv_sem=rsem.at[n],
            device_id=device, device_id_type=MESH,
        )

    barrier = pltpu.get_barrier_semaphore()

    def greet(i, carry):
        pl.semaphore_signal(
            barrier, inc=1, device_id=peer(lax.rem(chip + i, CHIPS)), device_id_type=MESH
        )
        return carry

    lax.fori_loop(1, CHIPS, greet, 0)
    for device in (to_mate, to_half):
        pl.semaphore_signal(barrier, inc=1, device_id=device, device_id_type=MESH)
    pl.semaphore_wait(barrier, CHIPS + 1)

    send_g = copy(g_ref, goth, 0, to_half)
    send_g.start()

    lane128 = iota((1, 128), 1)
    lane256 = iota((1, 256), 1)
    lane512 = iota((1, TOK), 1)
    row128 = iota((128, 1), 0)
    row16 = iota((16, 1), 0)
    pair16 = (row16 < 8) == (lane128 < HD)

    q2[...] = jnp.zeros_like(q2)
    do2[...] = jnp.zeros_like(do2)

    def pick(p, carry):
        q, k, v = q_ref[:, cols(p)], k_ref[:, cols(p)], v_ref[:, cols(p)]
        kv = jnp.concatenate([k, v], axis=1)
        rows, columns = iota((128, TOK), 0), iota((128, TOK), 1)
        hits = []
        for j in range(2):
            f1 = off_ref[0, first + 2 * p + j]
            hit = jnp.where(columns == rows * 4 + f1, 1.0, 0.0).astype(BF16)
            e1[2 * p + j] = hit
            hits.append(hit)
        f2 = jnp.where(row16 < 8, off_ref[1, first + 2 * p], off_ref[1, first + 2 * p + 1])
        hit2 = jnp.where(
            iota((16, TOK), 1) == lax.rem(iota((16, TOK), 0), 8) * 64 + f2, 1.0, 0.0
        ).astype(BF16)
        e2[p] = hit2
        left = lax.rem(lane256, 128) < HD
        picked = jnp.where(left, nn(hits[0], kv), nn(hits[1], kv)).astype(BF16)
        kv1[r, p, 0:128, :] = picked[:, 0:128]
        kv1[r, p, 128:256, :] = picked[:, 128:256]
        both = nn(hit2, kv)
        few = jnp.where(left, both[0:8], both[8:16])
        x2[core, chip, :, cols(p)] = jnp.concatenate([few[:, 0:128], few[:, 128:256]], axis=0).astype(BF16)
        q2[pl.ds(pl.multiple_of(p * 16, 16), 16), cols(p)] = jnp.where(pair16, nn(hit2, q), 0.0).astype(BF16)
        q_t = q.T
        qt[p] = q_t
        kt[p] = k.T
        vt[p] = v.T
        for j in range(2):
            mine = (row128 < HD) if j == 0 else (row128 >= HD)
            q1t[2 * p + j] = jnp.where(mine, nt(q_t, hits[j]), 0.0).astype(BF16)
        return carry

    lax.fori_loop(0, 3, pick, 0)

    send_a = copy(kv1.at[r], kv1.at[r], 2, to_facing)
    send_a.start()
    send_b = copy(kv1.at[r], kv1.at[r], 1, to_mate)
    send_b.start()

    def spread(i, carry):
        copy(x2.at[core, chip], x2.at[core, chip], 4, peer(lax.rem(chip + i, CHIPS))).start()
        return carry

    lax.fori_loop(1, CHIPS, spread, 0)

    def forward(keys, q_masked, v_t, width):
        scores = nn(keys, q_masked)
        top = jnp.max(scores, axis=0, keepdims=True)
        weights = jnp.exp2((scores - top) * SCALE).astype(BF16)
        out = nn(jnp.concatenate([v_t, jnp.ones((16, TOK), BF16)], axis=0), weights)
        return weights, out, top

    def masked(x_t, j):
        mine = (row128 < HD) if j == 0 else (row128 >= HD)
        return jnp.where(mine, x_t, jnp.zeros((), x_t.dtype))

    def near(p, carry):
        k, q_t, v_t = k_ref[:, cols(p)], qt[p], vt[p]
        for j in range(2):
            weights, out, top = forward(k, masked(q_t, j), v_t[HD * j : HD * (j + 1)], TOK)
            p0[2 * p + j] = weights
            o0[2 * p + j] = out[0:HD]
            st0[2 * p + j, 0:1] = top
            st0[2 * p + j, 1:2] = out[HD : HD + 1]
        return carry

    lax.fori_loop(0, 2, near, 0)
    arrived_a = copy(kv1.at[r_facing], kv1.at[r_facing], 2, to_facing)
    arrived_a.wait_recv()
    send_c = copy(kv1.at[r_facing], kv1.at[r_facing], 3, to_mate)
    send_c.start()
    lax.fori_loop(2, 3, near, 0)
    copy(x2.at[core, pl.ds(0, 31)], x2.at[core, pl.ds(0, 31)], 4, to_mate).wait_recv()
    send_d = copy(x2.at[core], x2.at[core], 5, to_mate)
    send_d.start()

    copy(kv1.at[r_mate], kv1.at[r_mate], 1, to_mate).wait_recv()
    copy(kv1.at[r_other], kv1.at[r_other], 3, to_mate).wait_recv()

    def middle(p, carry):
        keys = kv1[:, p, 0:128, :].reshape(TOK, 128)
        values = kv1[:, p, 128:256, :].reshape(TOK, 128)
        k1t[p] = keys.T
        v_t = values.T
        for j in range(2):
            weights, out, top = forward(keys, q1t[2 * p + j], v_t[HD * j : HD * (j + 1)], 128)
            p1[2 * p + j] = weights
            hi, lo = halves(out[0:HD])
            stats = jnp.concatenate(
                thirds(out[HD : HD + 1]) + thirds(top) + [jnp.zeros((10, 128), F32)], axis=0
            ).astype(BF16)
            wide = nn(jnp.concatenate([hi, lo, stats], axis=0), e1[2 * p + j])
            o1[2 * p + j] = wide[0:HD] + wide[HD : 2 * HD]
            st1[2 * p + j, 1:2] = jnp.sum(wide[128:131], axis=0, keepdims=True)
            st1[2 * p + j, 0:1] = jnp.sum(wide[131:134], axis=0, keepdims=True)
        return carry

    lax.fori_loop(0, 3, middle, 0)

    copy(x2.at[1 - core], x2.at[1 - core], 5, to_mate).wait_recv()
    own_head = iota((48, 384), 0) // 8 == iota((48, 384), 1) // HD
    xs = x2[...].reshape(1024, 384)
    scores = nt(q2[...], xs)
    scores = jnp.where(lax.rem(iota((1, 1024), 1), 16) < 8, scores, -1e30)
    top = jnp.max(scores, axis=1, keepdims=True)
    weights = jnp.exp2((scores - top) * SCALE).astype(BF16).astype(F32)
    p2[...] = weights
    o2[...] = jnp.where(own_head, nn(pltpu.roll(weights, 8, 1).astype(BF16), xs), 0.0)
    st2[0] = jnp.broadcast_to(top, (48, 128))
    st2[1] = jnp.broadcast_to(jnp.sum(weights, axis=1, keepdims=True), (48, 128))

    def expand2(part, hit2):
        hi, lo = halves(part)
        return tn(jnp.concatenate([hi, lo], axis=0), jnp.concatenate([hit2, hit2], axis=0))

    def merge(p, carry):
        hit2 = e2[p]
        hit2_wide = hit2.astype(F32)
        sixteen = pl.ds(pl.multiple_of(p * 16, 16), 16)
        far = expand2(o2[sixteen, cols(p)], hit2)
        top2 = hit2_wide * st2[0, sixteen, 0:1]
        sum2 = hit2_wide * st2[1, sixteen, 0:1]
        found = []
        for j in range(2):
            n = 2 * p + j
            eight = slice(8 * j, 8 * j + 8)
            chosen1 = lax.rem(lane512, 4) == off_ref[0, first + n]
            chosen2 = lax.rem(lane512, 64) == off_ref[1, first + n]
            m0, l0 = st0[n, 0:1], st0[n, 1:2]
            m1, l1 = jnp.where(chosen1, st1[n, 0:1], -1e30), st1[n, 1:2]
            m2 = jnp.where(chosen2, jnp.sum(top2[eight], axis=0, keepdims=True), -1e30)
            l2 = jnp.sum(sum2[eight], axis=0, keepdims=True)
            highest = jnp.maximum(m0, jnp.maximum(m1, m2))
            c0 = jnp.exp2((m0 - highest) * SCALE)
            c1 = jnp.exp2((m1 - highest) * SCALE)
            c2 = jnp.exp2((m2 - highest) * SCALE)
            over = 1.0 / (c0 * l0 + c1 * l1 + c2 * l2)
            g0, g1, g2 = c0 * over, c1 * over, c2 * over
            gs[n, 0:1] = g0
            gs[n, 1:2] = g1
            gs[n, 2:3] = g2
            found.append(g0 * o0[n] + g1 * o1[n] + g2 * far[HD * j : HD * (j + 1)])
        both = jnp.concatenate(found, axis=0)
        at[pl.ds(pl.multiple_of(p * 128, 128), 128), :] = both.astype(BF16)
        an[:, cols(p)] = both.T.astype(BF16)
        return carry

    lax.fori_loop(0, 3, merge, 0)

    own_cols = pl.ds(pl.multiple_of(h * 384, 128), 384)
    other_cols = pl.ds(pl.multiple_of((1 - h) * 384, 128), 384)
    mxs[...] = nn(an[...], w_ref[:, other_cols]).astype(BF16)
    send_m = copy(mxs, mxr, 6, to_half)
    send_m.start()

    copy(goth, goth, 0, to_half).wait_recv()

    mate_rows = pl.ds(pl.multiple_of((1 - core) * 192, 64), 192)
    own_rows = pl.ds(pl.multiple_of(core * 192, 64), 192)
    wps[pl.ds(h * 12, 12)] = nn(at[mate_rows, :], g_ref[...]).astype(BF16).reshape(12, 16, 384)
    wps[pl.ds((1 - h) * 12, 12)] = nn(at[mate_rows, :], goth[...]).astype(BF16).reshape(12, 16, 384)
    send_w = copy(wps, wmr, 7, to_mate)
    send_w.start()

    gt[...] = (nt(w_ref[:, own_cols], g_ref[...]) + nt(w_ref[:, other_cols], goth[...])).astype(BF16)

    def shares(p, carry):
        hit2 = e2[p]
        hit2_wide = hit2.astype(F32)
        sixteen = pl.ds(pl.multiple_of(p * 16, 16), 16)
        grads = []
        deltas = []
        for j in range(2):
            n = 2 * p + j
            own = pl.ds(pl.multiple_of(p * 128 + j * HD, HD), HD)
            grad = gt[own, :].astype(F32)
            delta = jnp.sum(grad * at[own, :].astype(F32), axis=0, keepdims=True)
            gs[n, 3:4] = delta
            weight = 0.125 * gs[n, 2:3]
            grads.append((grad * weight).astype(BF16))
            deltas.append(
                jnp.sum(hit2_wide[8 * j : 8 * j + 8] * (weight * delta), axis=1, keepdims=True)
            )
        few = nt(hit2, jnp.concatenate(grads, axis=0))
        do2[sixteen, cols(p)] = jnp.where(pair16, few, 0.0).astype(BF16)
        de2[sixteen, :] = jnp.broadcast_to(jnp.concatenate(deltas, axis=0), (16, 128))
        return carry

    lax.fori_loop(0, 3, shares, 0)

    xs = x2[...].reshape(1024, 384)
    weights = p2[...]
    grad_prob = pltpu.roll(nt(do2[...], xs), 1024 - 8, 1)
    dscore = weights * (grad_prob - de2[:, 0:1])
    dscore_b = dscore.astype(BF16)
    dq2[...] = jnp.where(own_head, nn(dscore_b, xs), 0.0)
    left_side = jnp.concatenate([dscore, 8.0 * pltpu.roll(weights, 8, 1)], axis=0).astype(BF16)
    dx[...] = tn(left_side, jnp.concatenate([q2[...], do2[...]], axis=0)).reshape(2, CHIPS, 16, 384)
    dxs[...] = dx[1 - core].astype(BF16)
    send_x = copy(dxs, dxm, 11, to_mate)
    send_x.start()

    wpo[pl.ds(h * 12, 12)] = nn(at[own_rows, :], g_ref[...]).reshape(12, 16, 384)
    wpo[pl.ds((1 - h) * 12, 12)] = nn(at[own_rows, :], goth[...]).reshape(12, 16, 384)
    copy(wmr, wmr, 7, to_mate).wait_recv()
    wrs[...] = (wpo[...] + wmr[...].astype(F32)).astype(BF16)
    owner = chip < OWNERS

    def reduce_w(i, carry):
        c = lax.rem(chip + i, OWNERS)

        @pl.when(c != chip)
        def _():
            copy(wrs.at[c], wrr.at[chip], 8, peer(c)).start()

        return carry

    lax.fori_loop(0, OWNERS, reduce_w, 0)

    def middle_back(p, carry):
        values = kv1[:, p, 128:256, :].reshape(TOK, 128)
        dscores, probs, q_all, g_all = [], [], [], []
        for j in range(2):
            n = 2 * p + j
            own = pl.ds(pl.multiple_of(p * 128 + j * HD, HD), HD)
            weight = 0.125 * gs[n, 1:2]
            grad = (gt[own, :].astype(F32) * weight).astype(BF16)
            stats = jnp.concatenate(
                thirds(weight * gs[n, 3:4]) + [jnp.zeros((13, TOK), F32)], axis=0
            ).astype(BF16)
            few = nt(jnp.concatenate([grad, stats], axis=0), e1[n])
            delta = jnp.sum(few[HD : HD + 3], axis=0, keepdims=True)
            nothing = jnp.zeros((HD, 128), BF16)
            part = few[0:HD].astype(BF16)
            grad_m = jnp.concatenate([part, nothing] if j == 0 else [nothing, part], axis=0)
            prob = p1[n]
            dscore = (prob.astype(F32) * (nn(values, grad_m) - delta)).astype(BF16)
            hi, lo = halves(nn(k1t[p, HD * j : HD * (j + 1), :], dscore))
            wide = nn(jnp.concatenate([hi, lo], axis=0), e1[n])
            dqx[n] = wide[0:HD] + wide[HD : 2 * HD]
            dscores.append(dscore)
            probs.append(prob)
            q_all.append(q1t[n])
            g_all.append(grad_m)
        grad_k = nt(jnp.concatenate(dscores, axis=1), jnp.concatenate(q_all, axis=1))
        grad_v = 8.0 * nt(jnp.concatenate(probs, axis=1), jnp.concatenate(g_all, axis=1))
        dk1[:, p, 0:128, :] = grad_k.reshape(4, 128, 128)
        dk1[:, p, 128:256, :] = grad_v.reshape(4, 128, 128)
        return carry

    lax.fori_loop(0, 3, middle_back, 0)
    dks[0] = dk1[r_mate].astype(BF16)
    dks[1] = dk1[r_other].astype(BF16)
    send_k = copy(dks, dkm, 13, to_mate)
    send_k.start()

    copy(dxm, dxm, 11, to_mate).wait_recv()
    dxb[...] = (dx[core] + dxm[...].astype(F32)).astype(BF16)

    def reduce_x(i, carry):
        c = lax.rem(chip + i, CHIPS)
        copy(dxb.at[c], xr.at[chip], 12, peer(c)).start()
        return carry

    lax.fori_loop(1, CHIPS, reduce_x, 0)

    copy(dkm, dkm, 13, to_mate).wait_recv()
    dkc[...] = (dk1[r_facing] + dkm[1].astype(F32)).astype(BF16)
    send_f = copy(dkc, dkr, 14, to_facing)
    send_f.start()

    def near_back(p, carry):
        k_t, q_t, v = kt[p], qt[p], v_ref[:, cols(p)]
        grad_k = jnp.zeros((TOK, 128), F32)
        grad_v = jnp.zeros((TOK, 128), F32)
        grad_q = []
        for j in range(2):
            n = 2 * p + j
            own = pl.ds(pl.multiple_of(p * 128 + j * HD, HD), HD)
            weight = 0.125 * gs[n, 0:1]
            grad = (gt[own, :].astype(F32) * weight).astype(BF16)
            nothing = jnp.zeros((HD, TOK), BF16)
            grad_m = jnp.concatenate([grad, nothing] if j == 0 else [nothing, grad], axis=0)
            prob = p0[n]
            dscore = (prob.astype(F32) * (nn(v, grad_m) - weight * gs[n, 3:4])).astype(BF16)
            grad_q.append(nn(k_t[HD * j : HD * (j + 1)], dscore) + dqx[n])
            grad_k = grad_k + nt(dscore, masked(q_t, j))
            grad_v = grad_v + nt(prob, grad_m)
        sixteen = pl.ds(pl.multiple_of(p * 16, 16), 16)
        total = jnp.concatenate(grad_q, axis=0) + expand2(dq2[sixteen, cols(p)], e2[p])
        dq_ref[:, cols(p)] = total.T.astype(BF16)
        dk0[p] = grad_k
        dv0[p] = 8.0 * grad_v
        return carry

    lax.fori_loop(0, 3, near_back, 0)

    @pl.when(owner)
    def _():
        wrr[chip] = wrs[chip]
        copy(wrr.at[pl.ds(0, 31)], wrr.at[pl.ds(0, 31)], 8, to_mate).wait_recv()
        wfull[core, chip] = jnp.sum(wrr[...].astype(F32), axis=0).astype(BF16)

        def give(i, carry):
            copy(wfull.at[core, chip], wfull.at[core, chip], 9, peer(lax.rem(chip + i, CHIPS))).start()
            return carry

        lax.fori_loop(1, CHIPS, give, 0)

    copy(mxr, mxr, 6, to_half).wait_recv()
    mixed_ref[...] = (nn(an[...], w_ref[:, own_cols]) + mxr[...].astype(F32)).astype(BF16)

    xr[chip] = dxb[chip]
    copy(xr.at[pl.ds(0, 31)], xr.at[pl.ds(0, 31)], 12, to_mate).wait_recv()
    far = jnp.sum(xr[...].astype(F32), axis=0)
    o2[0:16, :] = far
    copy(dkr, dkr, 14, to_facing).wait_recv()

    def finish(p, carry):
        left = lax.rem(lane256, 128) < HD
        near1 = dk1[r, p] + dkm[0, p].astype(F32) + dkr[p].astype(F32)
        near1 = jnp.concatenate([near1[0:128], near1[128:256]], axis=1)
        hit = jnp.concatenate([e1[2 * p], e1[2 * p + 1]], axis=0)
        near1 = jnp.concatenate([jnp.where(left, near1, 0.0), jnp.where(left, 0.0, near1)], axis=0)
        hi, lo = halves(near1)
        few = o2[0:16, cols(p)]
        few = jnp.concatenate([few[0:8], few[8:16]], axis=1)
        few = jnp.concatenate([jnp.where(left, few, 0.0), jnp.where(left, 0.0, few)], axis=0)
        total = tn(hit, hi) + tn(hit, lo) + expand2_right(few, e2[p])
        dk_ref[:, cols(p)] = (dk0[p] + total[:, 0:128]).astype(BF16)
        dv_ref[:, cols(p)] = (dv0[p] + total[:, 128:256]).astype(BF16)
        return carry

    def expand2_right(part, hit2):
        hi, lo = halves(part)
        return tn(jnp.concatenate([hit2, hit2], axis=0), jnp.concatenate([hi, lo], axis=0))

    lax.fori_loop(0, 3, finish, 0)

    def gathered(n_blocks):
        copy(wfull.at[core, pl.ds(0, n_blocks)], wfull.at[core, pl.ds(0, n_blocks)], 9, to_mate).wait_recv()
        copy(wrs.at[pl.ds(0, n_blocks)], wrs.at[pl.ds(0, n_blocks)], 8, to_mate).wait_send()

    @pl.when(owner)
    def _():
        gathered(OWNERS - 1)
        copy(wrr.at[pl.ds(0, 31)], wrr.at[pl.ds(0, 31)], 9, to_mate).wait_send()

    @pl.when(jnp.logical_not(owner))
    def _():
        gathered(OWNERS)

    send_e = copy(wfull.at[core], wfull.at[core], 10, to_mate)
    send_e.start()
    copy(wfull.at[1 - core], wfull.at[1 - core], 10, to_mate).wait_recv()
    for half in range(2):
        for side_cols in range(2):
            dw_ref[half * 192 : half * 192 + 192, side_cols * 384 : side_cols * 384 + 384] = (
                wfull[half, side_cols * 12 : side_cols * 12 + 12].reshape(192, 384).astype(F32)
            )

    for sent in (send_g, send_a, send_b, send_c, send_d, send_m, send_w, send_x, send_k, send_f, send_e):
        sent.wait_send()
    copy(x2.at[core, pl.ds(0, 31)], x2.at[core, pl.ds(0, 31)], 4, to_mate).wait_send()
    copy(dxb.at[pl.ds(0, 31)], dxb.at[pl.ds(0, 31)], 12, to_mate).wait_send()


def per_device(queries, keys, values, offsets, w_out, grad_mixed):
    vmem = pl.BlockSpec(memory_space=pltpu.VMEM)
    V = pltpu.VMEM
    block = jax.ShapeDtypeStruct((TOK, 384), BF16)
    scratch = [
        V((4, 3, 256, 128), BF16),
        V((2, CHIPS, 16, 384), BF16),
        V((TOK, 384), BF16),
        V((3, 128, TOK), BF16),
        V((3, 128, TOK), BF16),
        V((3, 128, TOK), BF16),
        V((3, 128, TOK), BF16),
        V((6, 128, 128), BF16),
        V((48, 384), BF16),
        V((6, 128, TOK), BF16),
        V((3, 16, TOK), BF16),
        V((6, TOK, TOK), BF16),
        V((6, TOK, 128), BF16),
        V((48, 1024), F32),
        V((6, HD, TOK), F32),
        V((6, HD, TOK), F32),
        V((48, 384), F32),
        V((6, 8, TOK), F32),
        V((6, 8, TOK), F32),
        V((2, 48, 128), F32),
        V((384, TOK), BF16),
        V((TOK, 384), BF16),
        V((6, 8, TOK), F32),
        V((384, TOK), BF16),
        V((TOK, 384), BF16),
        V((TOK, 384), BF16),
        V((OWNERS, 16, 384), BF16),
        V((OWNERS, 16, 384), F32),
        V((OWNERS, 16, 384), BF16),
        V((OWNERS, 16, 384), BF16),
        V((CHIPS, 16, 384), BF16),
        V((2, OWNERS, 16, 384), BF16),
        V((48, 384), BF16),
        V((48, 128), F32),
        V((2, CHIPS, 16, 384), F32),
        V((CHIPS, 16, 384), BF16),
        V((CHIPS, 16, 384), BF16),
        V((CHIPS, 16, 384), BF16),
        V((CHIPS, 16, 384), BF16),
        V((48, 384), F32),
        V((6, HD, TOK), F32),
        V((4, 3, 256, 128), F32),
        V((2, 3, 256, 128), BF16),
        V((2, 3, 256, 128), BF16),
        V((3, 256, 128), BF16),
        V((3, 256, 128), BF16),
        V((3, TOK, 128), F32),
        V((3, TOK, 128), F32),
        pltpu.SemaphoreType.DMA((15,)),
        pltpu.SemaphoreType.DMA((15,)),
    ]
    return pl.pallas_call(
        kernel,
        out_shape=(block, block, block, block, jax.ShapeDtypeStruct((384, 768), F32)),
        in_specs=[pl.BlockSpec(memory_space=pltpu.SMEM)] + [vmem] * 5,
        out_specs=(vmem,) * 5,
        scratch_shapes=scratch,
        compiler_params=pltpu.CompilerParams(
            collective_id=0, has_side_effects=True, vmem_limit_bytes=60 << 20
        ),
    )(offsets, queries, keys, values, w_out, grad_mixed)


def solution(mesh):
    in_specs = (
        P("seq", "head"),
        P("seq", "head"),
        P("seq", "head"),
        P(),
        P("head", None),
        P("seq", "head"),
    )
    out_specs = (
        P("seq", "head"),
        P("seq", "head"),
        P("seq", "head"),
        P("seq", "head"),
        P("head", None),
    )
    return jax.shard_map(
        per_device, mesh=mesh, in_specs=in_specs, out_specs=out_specs, check_vma=False
    )
```

```python
import math

import jax
import jax.numpy as jnp
from jax import lax
from jax.experimental import pallas as pl
from jax.experimental.pallas import tpu as pltpu
from jax.sharding import PartitionSpec as P

HD = 64
TOK = 512
CHIPS = 32
PLANE = 8
ROWS = 4
OWNERS = 6
SCALE = 0.125 * math.log2(math.e)
MESH = pl.DeviceIdType.MESH
F32 = jnp.float32
BF16 = jnp.bfloat16


def nn(a, b):
    return lax.dot_general(a, b, (((1,), (0,)), ((), ())), preferred_element_type=F32)


def nt(a, b):
    return lax.dot_general(a, b, (((1,), (1,)), ((), ())), preferred_element_type=F32)


def tn(a, b):
    return lax.dot_general(a, b, (((0,), (0,)), ((), ())), preferred_element_type=F32)


def iota(shape, dim):
    return lax.broadcasted_iota(jnp.int32, shape, dim)


def halves(x):
    hi = x.astype(BF16)
    return hi, (x - hi.astype(F32)).astype(BF16)


def thirds(x):
    hi = x.astype(BF16).astype(F32)
    mid = (x - hi).astype(BF16).astype(F32)
    return [hi, mid, x - hi - mid]


def kernel(
    off_ref, q_hbm, k_hbm, v_hbm, w_hbm, g_hbm,
    mixed_hbm, dq_hbm, dk_hbm, dv_hbm, dw_hbm,
    q_ref, k_ref, v_ref, w_ref, g_ref, mixed_ref, dq_ref, dk_ref, dv_ref, dw_ref,
    kv1, x2, goth, qt, kt, vt, k1t, q1t, q2, e1, e2, p0, p1, p2, o0, o1, o2,
    m0s, l0s, m1s, l1s, gs, ds, at, an, gt, mxs, mxr, wps, wpo, wmr, wrs, wyr, wy, wxr, wfull,
    do2, dx, dxs, dxm, dxb, xyr, xb, xr, dq2, dqx, dk1, dks, dkm, dkc, dkr,
    ssem, rsem, isem, osem,
):
    s = lax.axis_index("seq")
    h = lax.axis_index("head")
    chip, core = s // 2, lax.rem(s, 2)
    r = lax.rem(s, 4)
    mate = s + 1 - 2 * core
    side = lax.rem(chip, 2)
    facing = s + 2 - 4 * side
    r_mate = r + 1 - 2 * core
    r_facing = r + 2 - 4 * side
    r_other = r_mate + 2 - 4 * side
    first = h * 6
    row, place = chip // PLANE, lax.rem(chip, PLANE)
    owner = place < OWNERS
    own_row = pl.ds(row * PLANE, PLANE)
    to_mate, to_facing, to_half = (mate, h), (facing, h), (s, 1 - h)

    def peer(c):
        return (2 * c + core, h)

    def copy(src, dst, n, device):
        return pltpu.make_async_remote_copy(
            src_ref=src, dst_ref=dst, send_sem=ssem.at[n], recv_sem=rsem.at[n],
            device_id=device, device_id_type=MESH,
        )

    loads = [
        pltpu.make_async_copy(src, dst, isem.at[i])
        for i, (src, dst) in enumerate(
            ((k_hbm, k_ref), (v_hbm, v_ref), (q_hbm, q_ref), (g_hbm, g_ref), (w_hbm, w_ref))
        )
    ]
    for load in loads:
        load.start()

    barrier = pltpu.get_barrier_semaphore()

    in_plane = [peer(row * PLANE + lax.rem(place + i, PLANE)) for i in range(1, PLANE)]
    other_rows = [lax.rem(row + i, ROWS) for i in range(1, ROWS)]
    in_column = [peer(other * PLANE + place) for other in other_rows]
    for device in [to_mate, to_half] + in_plane + in_column:
        pl.semaphore_signal(barrier, inc=1, device_id=device, device_id_type=MESH)

    lane128 = iota((1, 128), 1)
    lane256 = iota((1, 256), 1)
    lane512 = iota((1, TOK), 1)
    row128 = iota((128, 1), 0)
    row16 = iota((16, 1), 0)
    row8 = iota((8, 1), 0)
    pair16 = (row16 < 8) == (lane128 < HD)
    first_lanes = lane256 < 128
    diagonal = (row128 < HD) == first_lanes
    left = lax.rem(lane256, 128) < HD
    PAIRS = range(3)

    def cols(p):
        return slice(p * 128, p * 128 + 128)

    q2[...] = jnp.zeros_like(q2)
    do2[...] = jnp.zeros_like(do2)
    ds[...] = jnp.zeros_like(ds)
    for stat in (m0s, l0s, m1s, l1s):
        stat[...] = jnp.ones_like(stat)
    hits = []
    hits2 = []
    f1 = jnp.zeros((8, 1), jnp.int32)
    f2 = jnp.zeros((8, 1), jnp.int32)
    for n in range(6):
        f1 = jnp.where(row8 == n, off_ref[0, first + n], f1)
        f2 = jnp.where(row8 == n, off_ref[1, first + n], f2)
    rows, columns = iota((128, TOK), 0), iota((128, TOK), 1)
    for p in PAIRS:
        hits.append(
            [
                jnp.where(columns == rows * 4 + off_ref[0, first + 2 * p + j], 1.0, 0.0).astype(BF16)
                for j in range(2)
            ]
        )
        f2p = jnp.where(row16 < 8, off_ref[1, first + 2 * p], off_ref[1, first + 2 * p + 1])
        hits2.append(
            jnp.where(
                iota((16, TOK), 1) == lax.rem(iota((16, TOK), 0), 8) * 64 + f2p, 1.0, 0.0
            ).astype(BF16)
        )
        e1[p, 0:128] = hits[p][0]
        e1[p, 128:256] = hits[p][1]
        e2[p * 16 : p * 16 + 16] = hits2[p]
    loads[0].wait()
    loads[1].wait()
    for p in PAIRS:
        kv = jnp.concatenate([k_ref[:, cols(p)], v_ref[:, cols(p)]], axis=1)
        both = nn(hits2[p], kv)
        few = jnp.where(left, both[0:8], both[8:16])
        x2[core, chip, :, cols(p)] = jnp.concatenate([few[:, 0:128], few[:, 128:256]], axis=0).astype(BF16)
        picked = jnp.where(left, nn(hits[p][0], kv), nn(hits[p][1], kv)).astype(BF16)
        kv1[r, p, 0:128, :] = picked[:, 0:128]
        kv1[r, p, 128:256, :] = picked[:, 128:256]

    pl.semaphore_wait(barrier, PLANE + ROWS)
    send_g = copy(g_hbm, goth, 0, to_half)

    own_block = x2.at[core, chip]
    for device in in_plane:
        copy(own_block, own_block, 4, device).start()
    send_a = copy(kv1.at[r], kv1.at[r], 2, to_facing)
    send_a.start()
    send_b = copy(kv1.at[r], kv1.at[r], 1, to_mate)
    send_b.start()

    send_g.start()
    loads[2].wait()
    for p in PAIRS:
        q = q_ref[:, cols(p)]
        q2[p * 16 : p * 16 + 16, cols(p)] = jnp.where(pair16, nn(hits2[p], q), 0.0).astype(BF16)
        qt[p] = q.T
        kt[p] = k_ref[:, cols(p)].T
        vt[p] = v_ref[:, cols(p)].T
        q1t[p] = jnp.where(diagonal, nt(qt[p], e1[p]), 0.0).astype(BF16)

    def masked(x_t, j):
        mine = (row128 < HD) if j == 0 else (row128 >= HD)
        return jnp.where(mine, x_t, jnp.zeros((), x_t.dtype))

    def near(p):
        k, q_t, v_t = k_ref[:, cols(p)], qt[p], vt[p]
        for j in range(2):
            n = 2 * p + j
            scores = nn(k, masked(q_t, j))
            top = jnp.max(scores, axis=0, keepdims=True)
            weights = jnp.exp2((scores - top) * SCALE).astype(BF16)
            out = nn(
                jnp.concatenate([v_t[HD * j : HD * (j + 1)], jnp.ones((16, TOK), BF16)], axis=0), weights
            )
            p0[n] = weights
            o0[p, HD * j : HD * (j + 1)] = out[0:HD]
            m0s[n : n + 1] = top
            l0s[n : n + 1] = out[HD : HD + 1]

    near(0)
    seven = x2.at[core, pl.ds(0, PLANE - 1)]
    copy(seven, seven, 4, to_mate).wait_recv()
    own_blocks = x2.at[core, own_row]
    for i, device in enumerate(in_column):
        copy(own_blocks, own_blocks, 15 + i, device).start()
    copy(own_blocks, own_blocks, 5, to_mate).start()
    near(1)
    copy(kv1.at[r_facing], kv1.at[r_facing], 2, to_facing).wait_recv()
    send_c = copy(kv1.at[r_facing], kv1.at[r_facing], 3, to_mate)
    send_c.start()
    near(2)
    for i in range(3):
        source = lax.rem(row + ROWS - 1 - i, ROWS)
        arrived = x2.at[core, pl.ds(source * PLANE, PLANE)]
        copy(arrived, arrived, 15 + i, to_mate).wait_recv()
        copy(arrived, arrived, 5, to_mate).start()

    copy(kv1.at[r_mate], kv1.at[r_mate], 1, to_mate).wait_recv()
    copy(kv1.at[r_other], kv1.at[r_other], 3, to_mate).wait_recv()

    keys = [kv1[:, p, 0:128, :].reshape(TOK, 128) for p in PAIRS]
    values = [kv1[:, p, 128:256, :].reshape(TOK, 128) for p in PAIRS]
    scores = [nn(keys[p], q1t[p]) for p in PAIRS]
    v_ts = [values[p].T for p in PAIRS]
    for p in PAIRS:
        k1t[p] = keys[p].T
    tops = [jnp.max(scores[p], axis=0, keepdims=True) for p in PAIRS]
    weights = [jnp.exp2((scores[p] - tops[p]) * SCALE).astype(BF16) for p in PAIRS]
    for p in PAIRS:
        p1[p] = weights[p]
    outs = [
        nn(jnp.concatenate([v_ts[p], jnp.ones((16, TOK), BF16)], axis=0), weights[p]) for p in PAIRS
    ]
    wides = []
    for p in PAIRS:
        hi, lo = halves(jnp.where(diagonal, outs[p][0:128], 0.0))
        stats = []
        for stat in (outs[p][128:129], tops[p]):
            for mine in (first_lanes, jnp.logical_not(first_lanes)):
                stats += thirds(jnp.where(mine, stat, 0.0))
        stats = jnp.concatenate(stats + [jnp.zeros((4, 256), F32)], axis=0).astype(BF16)
        wides.append(nn(jnp.concatenate([hi, lo, stats], axis=0), e1[p]))
    for p in PAIRS:
        wide = wides[p]
        o1[p] = wide[0:128] + wide[128:256]
        for j in range(2):
            n = 2 * p + j
            l1s[n : n + 1] = jnp.sum(wide[256 + 3 * j : 259 + 3 * j], axis=0, keepdims=True)
            m1s[n : n + 1] = jnp.sum(wide[262 + 3 * j : 265 + 3 * j], axis=0, keepdims=True)

    copy(x2.at[1 - core], x2.at[1 - core], 5, to_mate).wait_recv()
    own_head = iota((48, 384), 0) // 8 == iota((48, 384), 1) // HD
    xs = x2[...].reshape(1024, 384)
    scores2 = nt(q2[...], xs)
    scores2 = jnp.where(lax.rem(iota((1, 1024), 1), 16) < 8, scores2, -1e30)
    top2 = jnp.max(scores2, axis=1, keepdims=True)
    weights2 = jnp.exp2((scores2 - top2) * SCALE).astype(BF16).astype(F32)
    p2[...] = weights2
    o2[...] = jnp.where(own_head, nn(pltpu.roll(weights2, 8, 1).astype(BF16), xs), 0.0)
    sum2 = jnp.sum(weights2, axis=1, keepdims=True)

    def expand2(part, hit2):
        hi, lo = halves(part)
        return tn(jnp.concatenate([hi, lo], axis=0), jnp.concatenate([hit2, hit2], axis=0))

    def expand2_right(part, hit2):
        hi, lo = halves(part)
        return tn(jnp.concatenate([hit2, hit2], axis=0), jnp.concatenate([hi, lo], axis=0))

    lane48 = iota((48, 48), 1)
    same_head = iota((48, 48), 0) // 8 == lax.rem(lane48, 8)
    table = jnp.zeros((48, 48), F32)
    for t, piece in enumerate(thirds(top2) + thirds(sum2)):
        table = jnp.where(lane48 // 8 == t, piece, table)
    table = jnp.where(same_head, table, 0.0).astype(BF16)
    stats2 = tn(table, e2[...])
    m2 = stats2[0:8] + stats2[8:16] + stats2[16:24]
    l2 = stats2[24:32] + stats2[32:40] + stats2[40:48]
    m0, l0, l1 = m0s[...], l0s[...], l1s[...]
    m1 = jnp.where(lax.rem(lane512, 4) == f1, m1s[...], -1e30)
    m2 = jnp.where(lax.rem(lane512, 64) == f2, m2, -1e30)
    highest = jnp.maximum(m0, jnp.maximum(m1, m2))
    c0 = jnp.exp2((m0 - highest) * SCALE)
    c1 = jnp.exp2((m1 - highest) * SCALE)
    c2 = jnp.exp2((m2 - highest) * SCALE)
    over = 1.0 / (c0 * l0 + c1 * l1 + c2 * l2)
    g0, g1, g2 = c0 * over, c1 * over, c2 * over
    gs[0] = g0
    gs[1] = g1
    gs[2] = g2
    fars = [expand2(o2[p * 16 : p * 16 + 16, cols(p)], e2[p * 16 : p * 16 + 16]) for p in PAIRS]
    for p in PAIRS:
        found = []
        for j in range(2):
            n = 2 * p + j
            part = slice(HD * j, HD * (j + 1))
            found.append(
                g0[n : n + 1] * o0[p, part] + g1[n : n + 1] * o1[p, part] + g2[n : n + 1] * fars[p][part]
            )
        both = jnp.concatenate(found, axis=0)
        at[p * 128 : p * 128 + 128, :] = both.astype(BF16)
        an[:, cols(p)] = both.T.astype(BF16)

    loads[3].wait()
    loads[4].wait()
    own_cols = pl.ds(pl.multiple_of(h * 384, 128), 384)
    other_cols = pl.ds(pl.multiple_of((1 - h) * 384, 128), 384)
    mxs[...] = nn(an[...], w_ref[:, other_cols]).astype(BF16)
    send_m = copy(mxs, mxr, 6, to_half)
    send_m.start()

    mate_rows = pl.ds(pl.multiple_of((1 - core) * 192, 64), 192)
    own_rows = pl.ds(pl.multiple_of(core * 192, 64), 192)
    wps[pl.ds(h * 12, 12)] = nn(at[mate_rows, :], g_ref[...]).astype(BF16).reshape(12, 16, 384)
    wpo[pl.ds(h * 12, 12)] = nn(at[own_rows, :], g_ref[...]).reshape(12, 16, 384)
    copy(goth, goth, 0, to_half).wait_recv()
    wps[pl.ds((1 - h) * 12, 12)] = nn(at[mate_rows, :], goth[...]).astype(BF16).reshape(12, 16, 384)
    send_w = copy(wps, wmr, 7, to_mate)
    send_w.start()
    gt[...] = (nt(w_ref[:, own_cols], g_ref[...]) + nt(w_ref[:, other_cols], goth[...])).astype(BF16)
    wpo[pl.ds((1 - h) * 12, 12)] = nn(at[own_rows, :], goth[...]).reshape(12, 16, 384)

    for n in range(6):
        own = slice(HD * n, HD * (n + 1))
        ds[n : n + 1] = jnp.sum(
            gt[own, :].astype(F32) * at[own, :].astype(F32), axis=0, keepdims=True
        )
    gs[...] = 0.125 * gs[...]

    def weighted(level, p):
        return jnp.concatenate(
            [
                (gt[HD * n : HD * (n + 1), :].astype(F32) * gs[level, n : n + 1]).astype(BF16)
                for n in (2 * p, 2 * p + 1)
            ],
            axis=0,
        )

    shares2 = gs[2] * ds[...]
    deltas2 = []
    for p in PAIRS:
        sixteen = slice(p * 16, p * 16 + 16)
        do2[sixteen, cols(p)] = jnp.where(pair16, nt(e2[sixteen], weighted(2, p)), 0.0).astype(BF16)
        share = jnp.where(row16 < 8, shares2[2 * p : 2 * p + 1], shares2[2 * p + 1 : 2 * p + 2])
        deltas2.append(jnp.sum(e2[sixteen].astype(F32) * share, axis=1, keepdims=True))
    delta2 = jnp.concatenate(deltas2, axis=0)

    xs = x2[...].reshape(1024, 384)
    weights2 = p2[...]
    grad_prob2 = pltpu.roll(nt(do2[...], xs), 1024 - 8, 1)
    dscore2 = weights2 * (grad_prob2 - delta2)
    left_side = jnp.concatenate([dscore2, 8.0 * pltpu.roll(weights2, 8, 1)], axis=0).astype(BF16)
    dx[...] = tn(left_side, jnp.concatenate([q2[...], do2[...]], axis=0)).reshape(2, CHIPS, 16, 384)
    dxs[...] = dx[1 - core].astype(BF16)
    send_x = copy(dxs, dxm, 11, to_mate)
    send_x.start()
    dq2[...] = jnp.where(own_head, nn(dscore2.astype(BF16), xs), 0.0)

    copy(wmr, wmr, 7, to_mate).wait_recv()
    wrs[...] = (wpo[...] + wmr[...].astype(F32)).astype(BF16)

    for i, device in enumerate(in_column):
        copy(wrs.at[pl.ds(other_rows[i] * OWNERS, OWNERS)], wyr.at[row], 8, device).start()

    fews = []
    for p in PAIRS:
        share = gs[1] * ds[...]
        stats = jnp.concatenate(
            thirds(share[2 * p : 2 * p + 1]) + thirds(share[2 * p + 1 : 2 * p + 2])
            + [jnp.zeros((10, TOK), F32)],
            axis=0,
        ).astype(BF16)
        fews.append(nt(jnp.concatenate([weighted(1, p), stats], axis=0), e1[p]))
    grads = [jnp.where(diagonal, fews[p][0:128], 0.0).astype(BF16) for p in PAIRS]
    deltas = [
        jnp.where(
            first_lanes,
            jnp.sum(fews[p][128:131], axis=0, keepdims=True),
            jnp.sum(fews[p][131:134], axis=0, keepdims=True),
        )
        for p in PAIRS
    ]
    values = [kv1[:, p, 128:256, :].reshape(TOK, 128) for p in PAIRS]
    grad_probs = [nn(values[p], grads[p]) for p in PAIRS]
    dscores = [(p1[p].astype(F32) * (grad_probs[p] - deltas[p])).astype(BF16) for p in PAIRS]
    for p in PAIRS:
        dk1[:, p, 0:128, :] = nt(dscores[p], q1t[p]).reshape(4, 128, 128)
        dk1[:, p, 128:256, :] = (8.0 * nt(p1[p], grads[p])).reshape(4, 128, 128)
    dks[0] = dk1[r_mate].astype(BF16)
    dks[1] = dk1[r_other].astype(BF16)
    send_k = copy(dks, dkm, 13, to_mate)
    send_k.start()

    copy(dxm, dxm, 11, to_mate).wait_recv()
    dxb[...] = (dx[core] + dxm[...].astype(F32)).astype(BF16)

    for i, device in enumerate(in_column):
        copy(dxb.at[pl.ds(other_rows[i] * PLANE, PLANE)], xyr.at[row], 12, device).start()

    wyr[row] = wrs[pl.ds(row * OWNERS, OWNERS)]
    copy(wyr.at[pl.ds(0, 3)], wyr.at[pl.ds(0, 3)], 8, to_mate).wait_recv()
    wy[...] = jnp.sum(wyr[...].astype(F32), axis=0).astype(BF16)
    for k in range(OWNERS):

        @pl.when(place != k)
        def _():
            copy(wy.at[k], wxr.at[place], 18, peer(row * PLANE + k)).start()

    firsts = [nn(k1t[p], dscores[p]) for p in PAIRS]
    for p in PAIRS:
        hi, lo = halves(jnp.where(diagonal, firsts[p], 0.0))
        wide = nn(jnp.concatenate([hi, lo], axis=0), e1[p])
        dqx[p] = wide[0:128] + wide[128:256] + expand2(
            dq2[p * 16 : p * 16 + 16, cols(p)], e2[p * 16 : p * 16 + 16]
        )
    nears = []

    def near_back(p):
        k_t, q_t, v = kt[p], qt[p], v_ref[:, cols(p)]
        grad_k = jnp.zeros((TOK, 128), F32)
        grad_v = jnp.zeros((TOK, 128), F32)
        grad_q = []
        grad = weighted(0, p)
        share = gs[0] * ds[...]
        for j in range(2):
            n = 2 * p + j
            grad_m = masked(grad, j)
            prob = p0[n]
            dscore = (prob.astype(F32) * (nn(v, grad_m) - share[n : n + 1])).astype(BF16)
            grad_q.append(nn(k_t[HD * j : HD * (j + 1)], dscore))
            grad_k = grad_k + nt(dscore, masked(q_t, j))
            grad_v = grad_v + nt(prob, grad_m)
        dq_ref[:, cols(p)] = (jnp.concatenate(grad_q, axis=0) + dqx[p]).T.astype(BF16)
        nears.append((grad_k, 8.0 * grad_v))

    near_back(0)
    copy(dkm, dkm, 13, to_mate).wait_recv()
    dkc[...] = (dk1[r_facing] + dkm[1].astype(F32)).astype(BF16)
    send_f = copy(dkc, dkr, 14, to_facing)
    send_f.start()
    near_back(1)

    xyr[row] = dxb[own_row]
    copy(xyr.at[pl.ds(0, 3)], xyr.at[pl.ds(0, 3)], 12, to_mate).wait_recv()
    xb[...] = jnp.sum(xyr[...].astype(F32), axis=0).astype(BF16)
    for i, device in enumerate(in_plane):
        copy(xb.at[lax.rem(place + 1 + i, PLANE)], xr.at[place], 19, device).start()

    @pl.when(owner)
    def _():
        wxr[place] = wy[place]
        copy(wxr.at[pl.ds(0, 7)], wxr.at[pl.ds(0, 7)], 18, to_mate).wait_recv()
        result = wfull.at[core, row * OWNERS + place]
        result[...] = jnp.sum(wxr[...].astype(F32), axis=0).astype(BF16)
        for device in in_plane:
            copy(result, result, 9, device).start()

    near_back(2)

    def plane_done(n_blocks):
        some = wfull.at[core, pl.ds(0, n_blocks)]
        copy(some, some, 9, to_mate).wait_recv()
        copy(wy.at[pl.ds(0, n_blocks)], wy.at[pl.ds(0, n_blocks)], 18, to_mate).wait_send()

    @pl.when(owner)
    def _():
        plane_done(OWNERS - 1)

    @pl.when(jnp.logical_not(owner))
    def _():
        plane_done(OWNERS)

    own_w = wfull.at[core, pl.ds(row * OWNERS, OWNERS)]
    for i, device in enumerate(in_column):
        copy(own_w, own_w, 20 + i, device).start()
    copy(own_w, own_w, 10, to_mate).start()
    outputs = [
        pltpu.make_async_copy(src, dst, osem.at[i])
        for i, (src, dst) in enumerate(
            (
                (mixed_ref, mixed_hbm), (dq_ref, dq_hbm), (dk_ref, dk_hbm),
                (dv_ref, dv_hbm), (dw_ref, dw_hbm),
            )
        )
    ]
    outputs[1].start()

    own_part = nn(an[...], w_ref[:, own_cols])
    copy(mxr, mxr, 6, to_half).wait_recv()
    mixed_ref[...] = (own_part + mxr[...].astype(F32)).astype(BF16)
    outputs[0].start()

    xr[place] = xb[place]
    copy(xr.at[pl.ds(0, 7)], xr.at[pl.ds(0, 7)], 19, to_mate).wait_recv()
    far = jnp.sum(xr[...].astype(F32), axis=0)
    copy(dkr, dkr, 14, to_facing).wait_recv()
    for p in PAIRS:
        near1 = dk1[r, p] + dkm[0, p].astype(F32) + dkr[p].astype(F32)
        near1 = jnp.concatenate([near1[0:128], near1[128:256]], axis=1)
        near1 = jnp.concatenate([jnp.where(left, near1, 0.0), jnp.where(left, 0.0, near1)], axis=0)
        hi, lo = halves(near1)
        few = jnp.concatenate([far[0:8, cols(p)], far[8:16, cols(p)]], axis=1)
        few = jnp.concatenate([jnp.where(left, few, 0.0), jnp.where(left, 0.0, few)], axis=0)
        total = tn(e1[p], hi) + tn(e1[p], lo) + expand2_right(few, e2[p * 16 : p * 16 + 16])
        dk_ref[:, cols(p)] = (nears[p][0] + total[:, 0:128]).astype(BF16)
        dv_ref[:, cols(p)] = (nears[p][1] + total[:, 128:256]).astype(BF16)
    outputs[2].start()
    outputs[3].start()

    for i in range(3):
        source = lax.rem(row + ROWS - 1 - i, ROWS)
        arrived = wfull.at[core, pl.ds(source * OWNERS, OWNERS)]
        copy(arrived, arrived, 20 + i, to_mate).wait_recv()
        copy(arrived, arrived, 10, to_mate).start()

    def write_w(half):
        for side_cols in range(2):
            dw_ref[pl.ds(pl.multiple_of(half * 192, 64), 192), side_cols * 384 : side_cols * 384 + 384] = wfull[
                half, side_cols * 12 : side_cols * 12 + 12
            ].reshape(192, 384)

    write_w(core)
    copy(wfull.at[1 - core], wfull.at[1 - core], 10, to_mate).wait_recv()
    write_w(1 - core)
    outputs[4].start()

    for sent in (send_g, send_a, send_b, send_c, send_m, send_w, send_x, send_k, send_f):
        sent.wait_send()
    copy(seven, seven, 4, to_mate).wait_send()
    copy(x2.at[core], x2.at[core], 5, to_mate).wait_send()
    for i in range(3):
        copy(own_blocks, own_blocks, 15 + i, to_mate).wait_send()
        copy(own_w, own_w, 20 + i, to_mate).wait_send()
    copy(wyr.at[pl.ds(0, 3)], wyr.at[pl.ds(0, 3)], 8, to_mate).wait_send()
    copy(xyr.at[pl.ds(0, 3)], xyr.at[pl.ds(0, 3)], 12, to_mate).wait_send()
    copy(xr.at[pl.ds(0, 7)], xr.at[pl.ds(0, 7)], 19, to_mate).wait_send()
    copy(wfull.at[core], wfull.at[core], 10, to_mate).wait_send()

    @pl.when(owner)
    def _():
        copy(wxr.at[pl.ds(0, 7)], wxr.at[pl.ds(0, 7)], 9, to_mate).wait_send()

    for output in outputs:
        output.wait()


def deliver(*refs):
    sources, targets, buffers, wide = refs[0:5], refs[5:10], refs[10:15], refs[15]
    in_sems, out_sems = refs[16:18]
    parts = [(i, half) for i in range(5) for half in range(2)]

    def rows(i, half):
        count = sources[i].shape[0] // 2
        return pl.ds(half * count, count)

    ins = [
        pltpu.make_async_copy(sources[i].at[rows(i, k)], buffers[i].at[rows(i, k)], in_sems.at[i, k])
        for i, k in parts
    ]
    for one in ins:
        one.start()
    outs = []
    for (i, k), one in zip(parts, ins):
        one.wait()
        source = buffers[i]
        if i == 4:
            wide[rows(i, k), :] = source[rows(i, k), :].astype(F32)
            source = wide
        outs.append(
            pltpu.make_async_copy(source.at[rows(i, k)], targets[i].at[rows(i, k)], out_sems.at[i, k])
        )
        outs[-1].start()
    for one in outs:
        one.wait()


def per_device(queries, keys, values, offsets, w_out, grad_mixed):
    anywhere = pl.BlockSpec(memory_space=pl.ANY)
    V = pltpu.VMEM
    block = jax.ShapeDtypeStruct((TOK, 384), BF16)
    scratch = [V((TOK, 384), BF16)] * 3 + [V((384, 768), BF16)] + [V((TOK, 384), BF16)] * 5 + [
        V((384, 768), BF16),
        V((4, 3, 256, 128), BF16),
        V((2, CHIPS, 16, 384), BF16),
        V((TOK, 384), BF16),
        V((3, 128, TOK), BF16),
        V((3, 128, TOK), BF16),
        V((3, 128, TOK), BF16),
        V((3, 128, TOK), BF16),
        V((3, 128, 256), BF16),
        V((48, 384), BF16),
        V((3, 256, TOK), BF16),
        V((48, TOK), BF16),
        V((6, TOK, TOK), BF16),
        V((3, TOK, 256), BF16),
        V((48, 1024), F32),
        V((3, 128, TOK), F32),
        V((3, 128, TOK), F32),
        V((48, 384), F32),
        V((8, TOK), F32),
        V((8, TOK), F32),
        V((8, TOK), F32),
        V((8, TOK), F32),
        V((3, 8, TOK), F32),
        V((8, TOK), F32),
        V((384, TOK), BF16),
        V((TOK, 384), BF16),
        V((384, TOK), BF16),
        V((TOK, 384), BF16),
        V((TOK, 384), BF16),
        V((24, 16, 384), BF16),
        V((24, 16, 384), F32),
        V((24, 16, 384), BF16),
        V((24, 16, 384), BF16),
        V((ROWS, OWNERS, 16, 384), BF16),
        V((OWNERS, 16, 384), BF16),
        V((PLANE, 16, 384), BF16),
        V((2, 24, 16, 384), BF16),
        V((48, 384), BF16),
        V((2, CHIPS, 16, 384), F32),
        V((CHIPS, 16, 384), BF16),
        V((CHIPS, 16, 384), BF16),
        V((CHIPS, 16, 384), BF16),
        V((ROWS, PLANE, 16, 384), BF16),
        V((PLANE, 16, 384), BF16),
        V((PLANE, 16, 384), BF16),
        V((48, 384), F32),
        V((3, 128, TOK), F32),
        V((4, 3, 256, 128), F32),
        V((2, 3, 256, 128), BF16),
        V((2, 3, 256, 128), BF16),
        V((3, 256, 128), BF16),
        V((3, 256, 128), BF16),
        pltpu.SemaphoreType.DMA((23,)),
        pltpu.SemaphoreType.DMA((23,)),
        pltpu.SemaphoreType.DMA((5,)),
        pltpu.SemaphoreType.DMA((5,)),
    ]
    results = pl.pallas_call(
        kernel,
        out_shape=(block, block, block, block, jax.ShapeDtypeStruct((384, 768), BF16)),
        in_specs=[pl.BlockSpec(memory_space=pltpu.SMEM)] + [anywhere] * 5,
        out_specs=(anywhere,) * 5,
        scratch_shapes=scratch,
        compiler_params=pltpu.CompilerParams(
            collective_id=0, has_side_effects=True, vmem_limit_bytes=60 << 20
        ),
    )(offsets, queries, keys, values, w_out, grad_mixed)
    return pl.pallas_call(
        deliver,
        out_shape=(block, block, block, block, jax.ShapeDtypeStruct((384, 768), F32)),
        in_specs=[anywhere] * 5,
        out_specs=(anywhere,) * 5,
        scratch_shapes=[V((TOK, 384), BF16)] * 4 + [
            V((384, 768), BF16),
            V((384, 768), F32),
            pltpu.SemaphoreType.DMA((5, 2)),
            pltpu.SemaphoreType.DMA((5, 2)),
        ],
        compiler_params=pltpu.CompilerParams(vmem_limit_bytes=60 << 20),
    )(*results)


def solution(mesh):
    in_specs = (
        P("seq", "head"),
        P("seq", "head"),
        P("seq", "head"),
        P(),
        P("head", None),
        P("seq", "head"),
    )
    out_specs = (
        P("seq", "head"),
        P("seq", "head"),
        P("seq", "head"),
        P("seq", "head"),
        P("head", None),
    )
    return jax.shard_map(
        per_device, mesh=mesh, in_specs=in_specs, out_specs=out_specs, check_vma=False
    )
```

```python
import math

import jax
import jax.numpy as jnp
from jax import lax
from jax.experimental import pallas as pl
from jax.experimental.pallas import tpu as pltpu
from jax.sharding import PartitionSpec as P

HD = 64
TOK = 512
CHIPS = 32
PLANE = 8
ROWS = 4
OWNERS = 6
SCALE = 0.125 * math.log2(math.e)
MESH = pl.DeviceIdType.MESH
F32 = jnp.float32
BF16 = jnp.bfloat16


def nn(a, b):
    return lax.dot_general(a, b, (((1,), (0,)), ((), ())), preferred_element_type=F32)


def nt(a, b):
    return lax.dot_general(a, b, (((1,), (1,)), ((), ())), preferred_element_type=F32)


def tn(a, b):
    return lax.dot_general(a, b, (((0,), (0,)), ((), ())), preferred_element_type=F32)


def iota(shape, dim):
    return lax.broadcasted_iota(jnp.int32, shape, dim)


def halves(x):
    hi = x.astype(BF16)
    return hi, (x - hi.astype(F32)).astype(BF16)


def thirds(x):
    hi = x.astype(BF16).astype(F32)
    mid = (x - hi).astype(BF16).astype(F32)
    return [hi, mid, x - hi - mid]


def kernel(
    off_ref, q_hbm, k_hbm, v_hbm, w_hbm, g_hbm,
    mixed_hbm, dq_hbm, dk_hbm, dv_hbm, dw_hbm,
    q_ref, k_ref, v_ref, w_ref, g_ref, mixed_ref, dq_ref, dk_ref, dv_ref, dw_ref,
    kv1, x2, goth, qt, kt, vt, k1t, q1t, q2, e1, e2, p0, p1, p2, o0, o1, o2,
    m0s, l0s, m1s, l1s, gs, ds, at, an, gt, mxs, mxr, wps, wpo, wmr, wrs, wyr, wy, wxr, wfull,
    do2, dx, dxs, dxm, dxb, xyr, xb, xr, dq2, dqx, dk1, dks, dkm, dkc, dkr,
    ssem, rsem, isem, osem,
):
    s = lax.axis_index("seq")
    h = lax.axis_index("head")
    seat, core = s // 2, lax.rem(s, 2)
    x_at, z_at, y_at = lax.rem(seat, 4), lax.rem(seat // 4, 2), seat // 8
    r = lax.rem(s, 4)
    mate = s + 1 - 2 * core
    side = lax.rem(seat, 2)
    facing = s + 2 - 4 * side
    r_mate = r + 1 - 2 * core
    r_facing = r + 2 - 4 * side
    r_other = r_mate + 2 - 4 * side
    first = h * 6
    row = (1 - core) * y_at + core * x_at
    place = z_at * 4 + (1 - core) * x_at + core * y_at
    chip = row * PLANE + place
    owner = place < OWNERS
    own_row = pl.ds(row * PLANE, PLANE)
    to_mate, to_facing, to_half = (mate, h), (facing, h), (s, 1 - h)

    def peer(c):
        major, deep, minor = c // PLANE, lax.rem(c, PLANE) // 4, lax.rem(c, 4)
        y_to = (1 - core) * major + core * minor
        x_to = (1 - core) * minor + core * major
        return (2 * (y_to * 8 + deep * 4 + x_to) + core, h)

    def copy(src, dst, n, device):
        return pltpu.make_async_remote_copy(
            src_ref=src, dst_ref=dst, send_sem=ssem.at[n], recv_sem=rsem.at[n],
            device_id=device, device_id_type=MESH,
        )

    loads = [
        pltpu.make_async_copy(src, dst, isem.at[i])
        for i, (src, dst) in enumerate(
            ((k_hbm, k_ref), (v_hbm, v_ref), (q_hbm, q_ref), (g_hbm, g_ref), (w_hbm, w_ref))
        )
    ]
    for load in loads:
        load.start()

    barrier = pltpu.get_barrier_semaphore()

    in_plane = [peer(row * PLANE + lax.rem(place + i, PLANE)) for i in range(1, PLANE)]
    other_rows = [lax.rem(row + i, ROWS) for i in range(1, ROWS)]
    in_column = [peer(other * PLANE + place) for other in other_rows]
    for device in [to_mate, to_half] + in_plane + in_column:
        pl.semaphore_signal(barrier, inc=1, device_id=device, device_id_type=MESH)

    lane128 = iota((1, 128), 1)
    lane256 = iota((1, 256), 1)
    lane512 = iota((1, TOK), 1)
    row128 = iota((128, 1), 0)
    row16 = iota((16, 1), 0)
    row8 = iota((8, 1), 0)
    pair16 = (row16 < 8) == (lane128 < HD)
    first_lanes = lane256 < 128
    diagonal = (row128 < HD) == first_lanes
    left = lax.rem(lane256, 128) < HD
    PAIRS = range(3)

    def cols(p):
        return slice(p * 128, p * 128 + 128)

    q2[...] = jnp.zeros_like(q2)
    do2[...] = jnp.zeros_like(do2)
    ds[...] = jnp.zeros_like(ds)
    for stat in (m0s, l0s, m1s, l1s):
        stat[...] = jnp.ones_like(stat)
    hits = []
    hits2 = []
    f1 = jnp.zeros((8, 1), jnp.int32)
    f2 = jnp.zeros((8, 1), jnp.int32)
    for n in range(6):
        f1 = jnp.where(row8 == n, off_ref[0, first + n], f1)
        f2 = jnp.where(row8 == n, off_ref[1, first + n], f2)
    rows, columns = iota((128, TOK), 0), iota((128, TOK), 1)
    for p in PAIRS:
        hits.append(
            [
                jnp.where(columns == rows * 4 + off_ref[0, first + 2 * p + j], 1.0, 0.0).astype(BF16)
                for j in range(2)
            ]
        )
        f2p = jnp.where(row16 < 8, off_ref[1, first + 2 * p], off_ref[1, first + 2 * p + 1])
        hits2.append(
            jnp.where(
                iota((16, TOK), 1) == lax.rem(iota((16, TOK), 0), 8) * 64 + f2p, 1.0, 0.0
            ).astype(BF16)
        )
        e1[p, 0:128] = hits[p][0]
        e1[p, 128:256] = hits[p][1]
        e2[p * 16 : p * 16 + 16] = hits2[p]
    loads[0].wait()
    loads[1].wait()
    for p in PAIRS:
        kv = jnp.concatenate([k_ref[:, cols(p)], v_ref[:, cols(p)]], axis=1)
        both = nn(hits2[p], kv)
        few = jnp.where(left, both[0:8], both[8:16])
        x2[core, chip, :, cols(p)] = jnp.concatenate([few[:, 0:128], few[:, 128:256]], axis=0).astype(BF16)
        picked = jnp.where(left, nn(hits[p][0], kv), nn(hits[p][1], kv)).astype(BF16)
        kv1[r, p, 0:128, :] = picked[:, 0:128]
        kv1[r, p, 128:256, :] = picked[:, 128:256]

    pl.semaphore_wait(barrier, PLANE + ROWS)
    send_g = copy(g_hbm, goth, 0, to_half)

    own_block = x2.at[core, chip]
    for device in in_plane:
        copy(own_block, own_block, 4, device).start()
    send_a = copy(kv1.at[r], kv1.at[r], 2, to_facing)
    send_a.start()
    send_b = copy(kv1.at[r], kv1.at[r], 1, to_mate)
    send_b.start()

    send_g.start()
    loads[2].wait()
    for p in PAIRS:
        q = q_ref[:, cols(p)]
        q2[p * 16 : p * 16 + 16, cols(p)] = jnp.where(pair16, nn(hits2[p], q), 0.0).astype(BF16)
        qt[p] = q.T
        kt[p] = k_ref[:, cols(p)].T
        vt[p] = v_ref[:, cols(p)].T
        q1t[p] = jnp.where(diagonal, nt(qt[p], e1[p]), 0.0).astype(BF16)

    def masked(x_t, j):
        mine = (row128 < HD) if j == 0 else (row128 >= HD)
        return jnp.where(mine, x_t, jnp.zeros((), x_t.dtype))

    def near(p):
        k, q_t, v_t = k_ref[:, cols(p)], qt[p], vt[p]
        for j in range(2):
            n = 2 * p + j
            scores = nn(k, masked(q_t, j))
            top = jnp.max(scores, axis=0, keepdims=True)
            weights = jnp.exp2((scores - top) * SCALE).astype(BF16)
            out = nn(
                jnp.concatenate([v_t[HD * j : HD * (j + 1)], jnp.ones((16, TOK), BF16)], axis=0), weights
            )
            p0[n] = weights
            o0[p, HD * j : HD * (j + 1)] = out[0:HD]
            m0s[n : n + 1] = top
            l0s[n : n + 1] = out[HD : HD + 1]

    near(0)
    seven = x2.at[core, pl.ds(0, PLANE - 1)]
    copy(seven, seven, 4, to_mate).wait_recv()
    own_blocks = x2.at[core, own_row]
    for i, device in enumerate(in_column):
        copy(own_blocks, own_blocks, 15 + i, device).start()
    copy(own_blocks, own_blocks, 5, to_mate).start()
    near(1)
    copy(kv1.at[r_facing], kv1.at[r_facing], 2, to_facing).wait_recv()
    send_c = copy(kv1.at[r_facing], kv1.at[r_facing], 3, to_mate)
    send_c.start()
    near(2)
    for i in range(3):
        source = lax.rem(row + ROWS - 1 - i, ROWS)
        arrived = x2.at[core, pl.ds(source * PLANE, PLANE)]
        copy(arrived, arrived, 15 + i, to_mate).wait_recv()
        copy(arrived, arrived, 5, to_mate).start()

    copy(kv1.at[r_mate], kv1.at[r_mate], 1, to_mate).wait_recv()
    copy(kv1.at[r_other], kv1.at[r_other], 3, to_mate).wait_recv()

    keys = [kv1[:, p, 0:128, :].reshape(TOK, 128) for p in PAIRS]
    values = [kv1[:, p, 128:256, :].reshape(TOK, 128) for p in PAIRS]
    scores = [nn(keys[p], q1t[p]) for p in PAIRS]
    v_ts = [values[p].T for p in PAIRS]
    for p in PAIRS:
        k1t[p] = keys[p].T
    tops = [jnp.max(scores[p], axis=0, keepdims=True) for p in PAIRS]
    weights = [jnp.exp2((scores[p] - tops[p]) * SCALE).astype(BF16) for p in PAIRS]
    for p in PAIRS:
        p1[p] = weights[p]
    outs = [
        nn(jnp.concatenate([v_ts[p], jnp.ones((16, TOK), BF16)], axis=0), weights[p]) for p in PAIRS
    ]
    wides = []
    for p in PAIRS:
        hi, lo = halves(jnp.where(diagonal, outs[p][0:128], 0.0))
        stats = []
        for stat in (outs[p][128:129], tops[p]):
            for mine in (first_lanes, jnp.logical_not(first_lanes)):
                stats += thirds(jnp.where(mine, stat, 0.0))
        stats = jnp.concatenate(stats + [jnp.zeros((4, 256), F32)], axis=0).astype(BF16)
        wides.append(nn(jnp.concatenate([hi, lo, stats], axis=0), e1[p]))
    for p in PAIRS:
        wide = wides[p]
        o1[p] = wide[0:128] + wide[128:256]
        for j in range(2):
            n = 2 * p + j
            l1s[n : n + 1] = jnp.sum(wide[256 + 3 * j : 259 + 3 * j], axis=0, keepdims=True)
            m1s[n : n + 1] = jnp.sum(wide[262 + 3 * j : 265 + 3 * j], axis=0, keepdims=True)

    copy(x2.at[1 - core], x2.at[1 - core], 5, to_mate).wait_recv()
    own_head = iota((48, 384), 0) // 8 == iota((48, 384), 1) // HD
    xs = x2[...].reshape(1024, 384)
    scores2 = nt(q2[...], xs)
    scores2 = jnp.where(lax.rem(iota((1, 1024), 1), 16) < 8, scores2, -1e30)
    top2 = jnp.max(scores2, axis=1, keepdims=True)
    weights2 = jnp.exp2((scores2 - top2) * SCALE).astype(BF16).astype(F32)
    p2[...] = weights2
    o2[...] = jnp.where(own_head, nn(pltpu.roll(weights2, 8, 1).astype(BF16), xs), 0.0)
    sum2 = jnp.sum(weights2, axis=1, keepdims=True)

    def expand2(part, hit2):
        hi, lo = halves(part)
        return tn(jnp.concatenate([hi, lo], axis=0), jnp.concatenate([hit2, hit2], axis=0))

    def expand2_right(part, hit2):
        hi, lo = halves(part)
        return tn(jnp.concatenate([hit2, hit2], axis=0), jnp.concatenate([hi, lo], axis=0))

    lane48 = iota((48, 48), 1)
    same_head = iota((48, 48), 0) // 8 == lax.rem(lane48, 8)
    table = jnp.zeros((48, 48), F32)
    for t, piece in enumerate(thirds(top2) + thirds(sum2)):
        table = jnp.where(lane48 // 8 == t, piece, table)
    table = jnp.where(same_head, table, 0.0).astype(BF16)
    stats2 = tn(table, e2[...])
    m2 = stats2[0:8] + stats2[8:16] + stats2[16:24]
    l2 = stats2[24:32] + stats2[32:40] + stats2[40:48]
    m0, l0, l1 = m0s[...], l0s[...], l1s[...]
    m1 = jnp.where(lax.rem(lane512, 4) == f1, m1s[...], -1e30)
    m2 = jnp.where(lax.rem(lane512, 64) == f2, m2, -1e30)
    highest = jnp.maximum(m0, jnp.maximum(m1, m2))
    c0 = jnp.exp2((m0 - highest) * SCALE)
    c1 = jnp.exp2((m1 - highest) * SCALE)
    c2 = jnp.exp2((m2 - highest) * SCALE)
    over = 1.0 / (c0 * l0 + c1 * l1 + c2 * l2)
    g0, g1, g2 = c0 * over, c1 * over, c2 * over
    gs[0] = g0
    gs[1] = g1
    gs[2] = g2
    fars = [expand2(o2[p * 16 : p * 16 + 16, cols(p)], e2[p * 16 : p * 16 + 16]) for p in PAIRS]
    for p in PAIRS:
        found = []
        for j in range(2):
            n = 2 * p + j
            part = slice(HD * j, HD * (j + 1))
            found.append(
                g0[n : n + 1] * o0[p, part] + g1[n : n + 1] * o1[p, part] + g2[n : n + 1] * fars[p][part]
            )
        both = jnp.concatenate(found, axis=0)
        at[p * 128 : p * 128 + 128, :] = both.astype(BF16)
        an[:, cols(p)] = both.T.astype(BF16)

    loads[3].wait()
    loads[4].wait()
    own_cols = pl.ds(pl.multiple_of(h * 384, 128), 384)
    other_cols = pl.ds(pl.multiple_of((1 - h) * 384, 128), 384)
    mxs[...] = nn(an[...], w_ref[:, other_cols]).astype(BF16)
    send_m = copy(mxs, mxr, 6, to_half)
    send_m.start()

    mate_rows = pl.ds(pl.multiple_of((1 - core) * 192, 64), 192)
    own_rows = pl.ds(pl.multiple_of(core * 192, 64), 192)
    wps[pl.ds(h * 12, 12)] = nn(at[mate_rows, :], g_ref[...]).astype(BF16).reshape(12, 16, 384)
    wpo[pl.ds(h * 12, 12)] = nn(at[own_rows, :], g_ref[...]).reshape(12, 16, 384)
    copy(goth, goth, 0, to_half).wait_recv()
    wps[pl.ds((1 - h) * 12, 12)] = nn(at[mate_rows, :], goth[...]).astype(BF16).reshape(12, 16, 384)
    send_w = copy(wps, wmr, 7, to_mate)
    send_w.start()
    gt[...] = (nt(w_ref[:, own_cols], g_ref[...]) + nt(w_ref[:, other_cols], goth[...])).astype(BF16)
    wpo[pl.ds((1 - h) * 12, 12)] = nn(at[own_rows, :], goth[...]).reshape(12, 16, 384)

    for n in range(6):
        own = slice(HD * n, HD * (n + 1))
        ds[n : n + 1] = jnp.sum(
            gt[own, :].astype(F32) * at[own, :].astype(F32), axis=0, keepdims=True
        )
    gs[...] = 0.125 * gs[...]

    def weighted(level, p):
        return jnp.concatenate(
            [
                (gt[HD * n : HD * (n + 1), :].astype(F32) * gs[level, n : n + 1]).astype(BF16)
                for n in (2 * p, 2 * p + 1)
            ],
            axis=0,
        )

    shares2 = gs[2] * ds[...]
    deltas2 = []
    for p in PAIRS:
        sixteen = slice(p * 16, p * 16 + 16)
        do2[sixteen, cols(p)] = jnp.where(pair16, nt(e2[sixteen], weighted(2, p)), 0.0).astype(BF16)
        share = jnp.where(row16 < 8, shares2[2 * p : 2 * p + 1], shares2[2 * p + 1 : 2 * p + 2])
        deltas2.append(jnp.sum(e2[sixteen].astype(F32) * share, axis=1, keepdims=True))
    delta2 = jnp.concatenate(deltas2, axis=0)

    xs = x2[...].reshape(1024, 384)
    weights2 = p2[...]
    grad_prob2 = pltpu.roll(nt(do2[...], xs), 1024 - 8, 1)
    dscore2 = weights2 * (grad_prob2 - delta2)
    left_side = jnp.concatenate([dscore2, 8.0 * pltpu.roll(weights2, 8, 1)], axis=0).astype(BF16)
    dx[...] = tn(left_side, jnp.concatenate([q2[...], do2[...]], axis=0)).reshape(2, CHIPS, 16, 384)
    dxs[...] = dx[1 - core].astype(BF16)
    send_x = copy(dxs, dxm, 11, to_mate)
    send_x.start()
    dq2[...] = jnp.where(own_head, nn(dscore2.astype(BF16), xs), 0.0)

    copy(wmr, wmr, 7, to_mate).wait_recv()
    wrs[...] = (wpo[...] + wmr[...].astype(F32)).astype(BF16)

    for i, device in enumerate(in_column):
        copy(wrs.at[pl.ds(other_rows[i] * OWNERS, OWNERS)], wyr.at[row], 8, device).start()

    fews = []
    for p in PAIRS:
        share = gs[1] * ds[...]
        stats = jnp.concatenate(
            thirds(share[2 * p : 2 * p + 1]) + thirds(share[2 * p + 1 : 2 * p + 2])
            + [jnp.zeros((10, TOK), F32)],
            axis=0,
        ).astype(BF16)
        fews.append(nt(jnp.concatenate([weighted(1, p), stats], axis=0), e1[p]))
    grads = [jnp.where(diagonal, fews[p][0:128], 0.0).astype(BF16) for p in PAIRS]
    deltas = [
        jnp.where(
            first_lanes,
            jnp.sum(fews[p][128:131], axis=0, keepdims=True),
            jnp.sum(fews[p][131:134], axis=0, keepdims=True),
        )
        for p in PAIRS
    ]
    values = [kv1[:, p, 128:256, :].reshape(TOK, 128) for p in PAIRS]
    grad_probs = [nn(values[p], grads[p]) for p in PAIRS]
    dscores = [(p1[p].astype(F32) * (grad_probs[p] - deltas[p])).astype(BF16) for p in PAIRS]
    for p in PAIRS:
        dk1[:, p, 0:128, :] = nt(dscores[p], q1t[p]).reshape(4, 128, 128)
        dk1[:, p, 128:256, :] = (8.0 * nt(p1[p], grads[p])).reshape(4, 128, 128)
    dks[0] = dk1[r_mate].astype(BF16)
    dks[1] = dk1[r_other].astype(BF16)
    send_k = copy(dks, dkm, 13, to_mate)
    send_k.start()

    copy(dxm, dxm, 11, to_mate).wait_recv()
    dxb[...] = (dx[core] + dxm[...].astype(F32)).astype(BF16)

    for i, device in enumerate(in_column):
        copy(dxb.at[pl.ds(other_rows[i] * PLANE, PLANE)], xyr.at[row], 12, device).start()

    wyr[row] = wrs[pl.ds(row * OWNERS, OWNERS)]
    copy(wyr.at[pl.ds(0, 3)], wyr.at[pl.ds(0, 3)], 8, to_mate).wait_recv()
    wy[...] = jnp.sum(wyr[...].astype(F32), axis=0).astype(BF16)
    for k in range(OWNERS):

        @pl.when(place != k)
        def _():
            copy(wy.at[k], wxr.at[place], 18, peer(row * PLANE + k)).start()

    firsts = [nn(k1t[p], dscores[p]) for p in PAIRS]
    for p in PAIRS:
        hi, lo = halves(jnp.where(diagonal, firsts[p], 0.0))
        wide = nn(jnp.concatenate([hi, lo], axis=0), e1[p])
        dqx[p] = wide[0:128] + wide[128:256] + expand2(
            dq2[p * 16 : p * 16 + 16, cols(p)], e2[p * 16 : p * 16 + 16]
        )
    nears = []

    def near_back(p):
        k_t, q_t, v = kt[p], qt[p], v_ref[:, cols(p)]
        grad_k = jnp.zeros((TOK, 128), F32)
        grad_v = jnp.zeros((TOK, 128), F32)
        grad_q = []
        grad = weighted(0, p)
        share = gs[0] * ds[...]
        for j in range(2):
            n = 2 * p + j
            grad_m = masked(grad, j)
            prob = p0[n]
            dscore = (prob.astype(F32) * (nn(v, grad_m) - share[n : n + 1])).astype(BF16)
            grad_q.append(nn(k_t[HD * j : HD * (j + 1)], dscore))
            grad_k = grad_k + nt(dscore, masked(q_t, j))
            grad_v = grad_v + nt(prob, grad_m)
        dq_ref[:, cols(p)] = (jnp.concatenate(grad_q, axis=0) + dqx[p]).T.astype(BF16)
        nears.append((grad_k, 8.0 * grad_v))

    near_back(0)
    copy(dkm, dkm, 13, to_mate).wait_recv()
    dkc[...] = (dk1[r_facing] + dkm[1].astype(F32)).astype(BF16)
    send_f = copy(dkc, dkr, 14, to_facing)
    send_f.start()
    @pl.when(owner)
    def _():
        wxr[place] = wy[place]
        copy(wxr.at[pl.ds(0, 7)], wxr.at[pl.ds(0, 7)], 18, to_mate).wait_recv()
        result = wfull.at[core, row * OWNERS + place]
        result[...] = jnp.sum(wxr[...].astype(F32), axis=0).astype(BF16)
        for device in in_plane:
            copy(result, result, 9, device).start()

    near_back(1)

    xyr[row] = dxb[own_row]
    copy(xyr.at[pl.ds(0, 3)], xyr.at[pl.ds(0, 3)], 12, to_mate).wait_recv()
    xb[...] = jnp.sum(xyr[...].astype(F32), axis=0).astype(BF16)
    for i, device in enumerate(in_plane):
        copy(xb.at[lax.rem(place + 1 + i, PLANE)], xr.at[place], 19, device).start()

    def plane_done(n_blocks):
        some = wfull.at[core, pl.ds(0, n_blocks)]
        copy(some, some, 9, to_mate).wait_recv()
        copy(wy.at[pl.ds(0, n_blocks)], wy.at[pl.ds(0, n_blocks)], 18, to_mate).wait_send()

    @pl.when(owner)
    def _():
        plane_done(OWNERS - 1)

    @pl.when(jnp.logical_not(owner))
    def _():
        plane_done(OWNERS)

    own_w = wfull.at[core, pl.ds(row * OWNERS, OWNERS)]
    for i, device in enumerate(in_column):
        copy(own_w, own_w, 20 + i, device).start()
    copy(own_w, own_w, 10, to_mate).start()
    near_back(2)

    outputs = [
        pltpu.make_async_copy(src, dst, osem.at[i])
        for i, (src, dst) in enumerate(
            (
                (mixed_ref, mixed_hbm), (dq_ref, dq_hbm), (dk_ref, dk_hbm),
                (dv_ref, dv_hbm), (dw_ref, dw_hbm),
            )
        )
    ]
    outputs[1].start()

    own_part = nn(an[...], w_ref[:, own_cols])
    copy(mxr, mxr, 6, to_half).wait_recv()
    mixed_ref[...] = (own_part + mxr[...].astype(F32)).astype(BF16)
    outputs[0].start()

    xr[place] = xb[place]
    copy(xr.at[pl.ds(0, 7)], xr.at[pl.ds(0, 7)], 19, to_mate).wait_recv()
    far = jnp.sum(xr[...].astype(F32), axis=0)
    copy(dkr, dkr, 14, to_facing).wait_recv()
    for p in PAIRS:
        near1 = dk1[r, p] + dkm[0, p].astype(F32) + dkr[p].astype(F32)
        near1 = jnp.concatenate([near1[0:128], near1[128:256]], axis=1)
        near1 = jnp.concatenate([jnp.where(left, near1, 0.0), jnp.where(left, 0.0, near1)], axis=0)
        hi, lo = halves(near1)
        few = jnp.concatenate([far[0:8, cols(p)], far[8:16, cols(p)]], axis=1)
        few = jnp.concatenate([jnp.where(left, few, 0.0), jnp.where(left, 0.0, few)], axis=0)
        total = tn(e1[p], hi) + tn(e1[p], lo) + expand2_right(few, e2[p * 16 : p * 16 + 16])
        dk_ref[:, cols(p)] = (nears[p][0] + total[:, 0:128]).astype(BF16)
        dv_ref[:, cols(p)] = (nears[p][1] + total[:, 128:256]).astype(BF16)
    outputs[2].start()
    outputs[3].start()

    for i in range(3):
        source = lax.rem(row + ROWS - 1 - i, ROWS)
        arrived = wfull.at[core, pl.ds(source * OWNERS, OWNERS)]
        copy(arrived, arrived, 20 + i, to_mate).wait_recv()
        copy(arrived, arrived, 10, to_mate).start()

    def write_w(half):
        for side_cols in range(2):
            dw_ref[pl.ds(pl.multiple_of(half * 192, 64), 192), side_cols * 384 : side_cols * 384 + 384] = wfull[
                half, side_cols * 12 : side_cols * 12 + 12
            ].reshape(192, 384)

    write_w(core)
    copy(wfull.at[1 - core], wfull.at[1 - core], 10, to_mate).wait_recv()
    write_w(1 - core)
    outputs[4].start()

    for sent in (send_g, send_a, send_b, send_c, send_m, send_w, send_x, send_k, send_f):
        sent.wait_send()
    copy(seven, seven, 4, to_mate).wait_send()
    copy(x2.at[core], x2.at[core], 5, to_mate).wait_send()
    for i in range(3):
        copy(own_blocks, own_blocks, 15 + i, to_mate).wait_send()
        copy(own_w, own_w, 20 + i, to_mate).wait_send()
    copy(wyr.at[pl.ds(0, 3)], wyr.at[pl.ds(0, 3)], 8, to_mate).wait_send()
    copy(xyr.at[pl.ds(0, 3)], xyr.at[pl.ds(0, 3)], 12, to_mate).wait_send()
    copy(xr.at[pl.ds(0, 7)], xr.at[pl.ds(0, 7)], 19, to_mate).wait_send()
    copy(wfull.at[core], wfull.at[core], 10, to_mate).wait_send()

    @pl.when(owner)
    def _():
        copy(wxr.at[pl.ds(0, 7)], wxr.at[pl.ds(0, 7)], 9, to_mate).wait_send()

    for output in outputs:
        output.wait()


def deliver(*refs):
    sources, targets, buffers, wide = refs[0:5], refs[5:10], refs[10:15], refs[15]
    in_sems, out_sems = refs[16:18]
    parts = [(i, half) for i in range(5) for half in range(2)]

    def rows(i, half):
        count = sources[i].shape[0] // 2
        return pl.ds(half * count, count)

    ins = [
        pltpu.make_async_copy(sources[i].at[rows(i, k)], buffers[i].at[rows(i, k)], in_sems.at[i, k])
        for i, k in parts
    ]
    for one in ins:
        one.start()
    outs = []
    for (i, k), one in zip(parts, ins):
        one.wait()
        source = buffers[i]
        if i == 4:
            wide[rows(i, k), :] = source[rows(i, k), :].astype(F32)
            source = wide
        outs.append(
            pltpu.make_async_copy(source.at[rows(i, k)], targets[i].at[rows(i, k)], out_sems.at[i, k])
        )
        outs[-1].start()
    for one in outs:
        one.wait()


def per_device(queries, keys, values, offsets, w_out, grad_mixed):
    anywhere = pl.BlockSpec(memory_space=pl.ANY)
    V = pltpu.VMEM
    block = jax.ShapeDtypeStruct((TOK, 384), BF16)
    scratch = [V((TOK, 384), BF16)] * 3 + [V((384, 768), BF16)] + [V((TOK, 384), BF16)] * 5 + [
        V((384, 768), BF16),
        V((4, 3, 256, 128), BF16),
        V((2, CHIPS, 16, 384), BF16),
        V((TOK, 384), BF16),
        V((3, 128, TOK), BF16),
        V((3, 128, TOK), BF16),
        V((3, 128, TOK), BF16),
        V((3, 128, TOK), BF16),
        V((3, 128, 256), BF16),
        V((48, 384), BF16),
        V((3, 256, TOK), BF16),
        V((48, TOK), BF16),
        V((6, TOK, TOK), BF16),
        V((3, TOK, 256), BF16),
        V((48, 1024), F32),
        V((3, 128, TOK), F32),
        V((3, 128, TOK), F32),
        V((48, 384), F32),
        V((8, TOK), F32),
        V((8, TOK), F32),
        V((8, TOK), F32),
        V((8, TOK), F32),
        V((3, 8, TOK), F32),
        V((8, TOK), F32),
        V((384, TOK), BF16),
        V((TOK, 384), BF16),
        V((384, TOK), BF16),
        V((TOK, 384), BF16),
        V((TOK, 384), BF16),
        V((24, 16, 384), BF16),
        V((24, 16, 384), F32),
        V((24, 16, 384), BF16),
        V((24, 16, 384), BF16),
        V((ROWS, OWNERS, 16, 384), BF16),
        V((OWNERS, 16, 384), BF16),
        V((PLANE, 16, 384), BF16),
        V((2, 24, 16, 384), BF16),
        V((48, 384), BF16),
        V((2, CHIPS, 16, 384), F32),
        V((CHIPS, 16, 384), BF16),
        V((CHIPS, 16, 384), BF16),
        V((CHIPS, 16, 384), BF16),
        V((ROWS, PLANE, 16, 384), BF16),
        V((PLANE, 16, 384), BF16),
        V((PLANE, 16, 384), BF16),
        V((48, 384), F32),
        V((3, 128, TOK), F32),
        V((4, 3, 256, 128), F32),
        V((2, 3, 256, 128), BF16),
        V((2, 3, 256, 128), BF16),
        V((3, 256, 128), BF16),
        V((3, 256, 128), BF16),
        pltpu.SemaphoreType.DMA((23,)),
        pltpu.SemaphoreType.DMA((23,)),
        pltpu.SemaphoreType.DMA((5,)),
        pltpu.SemaphoreType.DMA((5,)),
    ]
    results = pl.pallas_call(
        kernel,
        out_shape=(block, block, block, block, jax.ShapeDtypeStruct((384, 768), BF16)),
        in_specs=[pl.BlockSpec(memory_space=pltpu.SMEM)] + [anywhere] * 5,
        out_specs=(anywhere,) * 5,
        scratch_shapes=scratch,
        compiler_params=pltpu.CompilerParams(
            collective_id=0, has_side_effects=True, vmem_limit_bytes=60 << 20
        ),
    )(offsets, queries, keys, values, w_out, grad_mixed)
    return pl.pallas_call(
        deliver,
        out_shape=(block, block, block, block, jax.ShapeDtypeStruct((384, 768), F32)),
        in_specs=[anywhere] * 5,
        out_specs=(anywhere,) * 5,
        scratch_shapes=[V((TOK, 384), BF16)] * 4 + [
            V((384, 768), BF16),
            V((384, 768), F32),
            pltpu.SemaphoreType.DMA((5, 2)),
            pltpu.SemaphoreType.DMA((5, 2)),
        ],
        compiler_params=pltpu.CompilerParams(vmem_limit_bytes=60 << 20),
    )(*results)


def solution(mesh):
    in_specs = (
        P("seq", "head"),
        P("seq", "head"),
        P("seq", "head"),
        P(),
        P("head", None),
        P("seq", "head"),
    )
    out_specs = (
        P("seq", "head"),
        P("seq", "head"),
        P("seq", "head"),
        P("seq", "head"),
        P("head", None),
    )
    return jax.shard_map(
        per_device, mesh=mesh, in_specs=in_specs, out_specs=out_specs, check_vma=False
    )
```

```python
import math

import jax
import jax.numpy as jnp
from jax import lax
from jax.experimental import pallas as pl
from jax.experimental.pallas import tpu as pltpu
from jax.sharding import PartitionSpec as P

HD = 64
TOK = 512
CHIPS = 32
PLANE = 8
ROWS = 4
OWNERS = 6
SCALE = 0.125 * math.log2(math.e)
MESH = pl.DeviceIdType.MESH
F32 = jnp.float32
BF16 = jnp.bfloat16


def nn(a, b):
    return lax.dot_general(a, b, (((1,), (0,)), ((), ())), preferred_element_type=F32)


def nt(a, b):
    return lax.dot_general(a, b, (((1,), (1,)), ((), ())), preferred_element_type=F32)


def tn(a, b):
    return lax.dot_general(a, b, (((0,), (0,)), ((), ())), preferred_element_type=F32)


def iota(shape, dim):
    return lax.broadcasted_iota(jnp.int32, shape, dim)


def halves(x):
    hi = x.astype(BF16)
    return hi, (x - hi.astype(F32)).astype(BF16)


def thirds(x):
    hi = x.astype(BF16).astype(F32)
    mid = (x - hi).astype(BF16).astype(F32)
    return [hi, mid, x - hi - mid]


def kernel(
    off_ref, q_hbm, k_hbm, v_hbm, w_hbm, g_hbm,
    mixed_hbm, dq_hbm, dk_hbm, dv_hbm, dw_hbm,
    q_ref, k_ref, v_ref, w_ref, g_ref, mixed_ref, dq_ref, dk_ref, dv_ref, dw_ref,
    kv1, x2, goth, qt, kt, vt, k1t, q1t, q2, e1, e2, p0, p1, p2, o0, o1, o2,
    m0s, l0s, m1s, l1s, gs, ds, at, an, gt, mxs, mxr, wps, wpo, wmr, wrs, wyr, wy, wxr, wfull,
    do2, dx, dxs, dxm, dxb, xyr, xb, xr, dq2, dqx, dk1, dks, dkm, dkc, dkr,
    ssem, rsem, isem, osem,
):
    s = lax.axis_index("seq")
    h = lax.axis_index("head")
    seat, core = s // 2, lax.rem(s, 2)
    x_at, z_at, y_at = lax.rem(seat, 4), lax.rem(seat // 4, 2), seat // 8
    r = lax.rem(s, 4)
    mate = s + 1 - 2 * core
    side = lax.rem(seat, 2)
    facing = s + 2 - 4 * side
    r_mate = r + 1 - 2 * core
    r_facing = r + 2 - 4 * side
    r_other = r_mate + 2 - 4 * side
    first = h * 6
    row = (1 - core) * y_at + core * x_at
    place = z_at * 4 + (1 - core) * x_at + core * y_at
    chip = row * PLANE + place
    owner = place < OWNERS
    own_row = pl.ds(row * PLANE, PLANE)
    to_mate, to_facing, to_half = (mate, h), (facing, h), (s, 1 - h)

    def peer(c):
        major, deep, minor = c // PLANE, lax.rem(c, PLANE) // 4, lax.rem(c, 4)
        y_to = (1 - core) * major + core * minor
        x_to = (1 - core) * minor + core * major
        return (2 * (y_to * 8 + deep * 4 + x_to) + core, h)

    def copy(src, dst, n, device):
        return pltpu.make_async_remote_copy(
            src_ref=src, dst_ref=dst, send_sem=ssem.at[n], recv_sem=rsem.at[n],
            device_id=device, device_id_type=MESH,
        )

    loads = [
        pltpu.make_async_copy(src, dst, isem.at[i])
        for i, (src, dst) in enumerate(
            ((k_hbm, k_ref), (v_hbm, v_ref), (q_hbm, q_ref), (g_hbm, g_ref), (w_hbm, w_ref))
        )
    ]
    for load in loads:
        load.start()

    barrier = pltpu.get_barrier_semaphore()

    in_plane = [peer(row * PLANE + lax.rem(place + i, PLANE)) for i in range(1, PLANE)]
    other_rows = [lax.rem(row + i, ROWS) for i in range(1, ROWS)]
    in_column = [peer(other * PLANE + place) for other in other_rows]
    for device in [to_mate, to_half] + in_plane + in_column:
        pl.semaphore_signal(barrier, inc=1, device_id=device, device_id_type=MESH)

    lane128 = iota((1, 128), 1)
    lane256 = iota((1, 256), 1)
    lane512 = iota((1, TOK), 1)
    row128 = iota((128, 1), 0)
    row16 = iota((16, 1), 0)
    row8 = iota((8, 1), 0)
    pair16 = (row16 < 8) == (lane128 < HD)
    first_lanes = lane256 < 128
    diagonal = (row128 < HD) == first_lanes
    left = lax.rem(lane256, 128) < HD
    PAIRS = range(3)

    def cols(p):
        return slice(p * 128, p * 128 + 128)

    q2[...] = jnp.zeros_like(q2)
    do2[...] = jnp.zeros_like(do2)
    ds[...] = jnp.zeros_like(ds)
    for stat in (m0s, l0s, m1s, l1s):
        stat[...] = jnp.ones_like(stat)
    hits = []
    hits2 = []
    f1 = jnp.zeros((8, 1), jnp.int32)
    f2 = jnp.zeros((8, 1), jnp.int32)
    for n in range(6):
        f1 = jnp.where(row8 == n, off_ref[0, first + n], f1)
        f2 = jnp.where(row8 == n, off_ref[1, first + n], f2)
    rows, columns = iota((128, TOK), 0), iota((128, TOK), 1)
    for p in PAIRS:
        hits.append(
            [
                jnp.where(columns == rows * 4 + off_ref[0, first + 2 * p + j], 1.0, 0.0).astype(BF16)
                for j in range(2)
            ]
        )
        f2p = jnp.where(row16 < 8, off_ref[1, first + 2 * p], off_ref[1, first + 2 * p + 1])
        hits2.append(
            jnp.where(
                iota((16, TOK), 1) == lax.rem(iota((16, TOK), 0), 8) * 64 + f2p, 1.0, 0.0
            ).astype(BF16)
        )
        e1[p, 0:128] = hits[p][0]
        e1[p, 128:256] = hits[p][1]
        e2[p * 16 : p * 16 + 16] = hits2[p]
    loads[0].wait()
    loads[1].wait()
    for p in PAIRS:
        kv = jnp.concatenate([k_ref[:, cols(p)], v_ref[:, cols(p)]], axis=1)
        both = nn(hits2[p], kv)
        few = jnp.where(left, both[0:8], both[8:16])
        x2[core, chip, :, cols(p)] = jnp.concatenate([few[:, 0:128], few[:, 128:256]], axis=0).astype(BF16)
        picked = jnp.where(left, nn(hits[p][0], kv), nn(hits[p][1], kv)).astype(BF16)
        kv1[r, p, 0:128, :] = picked[:, 0:128]
        kv1[r, p, 128:256, :] = picked[:, 128:256]

    pl.semaphore_wait(barrier, PLANE + ROWS)
    send_g = copy(g_hbm, goth, 0, to_half)

    own_block = x2.at[core, chip]
    for device in in_plane:
        copy(own_block, own_block, 4, device).start()
    send_a = copy(kv1.at[r], kv1.at[r], 2, to_facing)
    send_a.start()
    send_b = copy(kv1.at[r], kv1.at[r], 1, to_mate)
    send_b.start()

    send_g.start()
    loads[2].wait()
    for p in PAIRS:
        q = q_ref[:, cols(p)]
        q2[p * 16 : p * 16 + 16, cols(p)] = jnp.where(pair16, nn(hits2[p], q), 0.0).astype(BF16)
        qt[p] = q.T
        kt[p] = k_ref[:, cols(p)].T
        vt[p] = v_ref[:, cols(p)].T
        q1t[p] = jnp.where(diagonal, nt(qt[p], e1[p]), 0.0).astype(BF16)

    def masked(x_t, j):
        mine = (row128 < HD) if j == 0 else (row128 >= HD)
        return jnp.where(mine, x_t, jnp.zeros((), x_t.dtype))

    def near(p):
        k, q_t, v_t = k_ref[:, cols(p)], qt[p], vt[p]
        for j in range(2):
            n = 2 * p + j
            scores = nn(k, masked(q_t, j))
            top = jnp.max(scores, axis=0, keepdims=True)
            weights = jnp.exp2((scores - top) * SCALE).astype(BF16)
            out = nn(
                jnp.concatenate([v_t[HD * j : HD * (j + 1)], jnp.ones((16, TOK), BF16)], axis=0), weights
            )
            p0[n] = weights
            o0[p, HD * j : HD * (j + 1)] = out[0:HD]
            m0s[n : n + 1] = top
            l0s[n : n + 1] = out[HD : HD + 1]

    near(0)
    seven = x2.at[core, pl.ds(0, PLANE - 1)]
    copy(seven, seven, 4, to_mate).wait_recv()
    own_blocks = x2.at[core, own_row]
    for i, device in enumerate(in_column):
        copy(own_blocks, own_blocks, 15 + i, device).start()
    copy(own_blocks, own_blocks, 5, to_mate).start()
    near(1)
    copy(kv1.at[r_facing], kv1.at[r_facing], 2, to_facing).wait_recv()
    send_c = copy(kv1.at[r_facing], kv1.at[r_facing], 3, to_mate)
    send_c.start()
    near(2)
    for i in range(3):
        source = lax.rem(row + ROWS - 1 - i, ROWS)
        arrived = x2.at[core, pl.ds(source * PLANE, PLANE)]
        copy(arrived, arrived, 15 + i, to_mate).wait_recv()
        copy(arrived, arrived, 5, to_mate).start()

    copy(kv1.at[r_mate], kv1.at[r_mate], 1, to_mate).wait_recv()
    copy(kv1.at[r_other], kv1.at[r_other], 3, to_mate).wait_recv()

    keys = [kv1[:, p, 0:128, :].reshape(TOK, 128) for p in PAIRS]
    values = [kv1[:, p, 128:256, :].reshape(TOK, 128) for p in PAIRS]
    scores = [nn(keys[p], q1t[p]) for p in PAIRS]
    v_ts = [values[p].T for p in PAIRS]
    for p in PAIRS:
        k1t[p] = keys[p].T
    tops = [jnp.max(scores[p], axis=0, keepdims=True) for p in PAIRS]
    weights = [jnp.exp2((scores[p] - tops[p]) * SCALE).astype(BF16) for p in PAIRS]
    for p in PAIRS:
        p1[p] = weights[p]
    outs = [
        nn(jnp.concatenate([v_ts[p], jnp.ones((16, TOK), BF16)], axis=0), weights[p]) for p in PAIRS
    ]
    wides = []
    for p in PAIRS:
        hi, lo = halves(jnp.where(diagonal, outs[p][0:128], 0.0))
        stats = []
        for stat in (outs[p][128:129], tops[p]):
            for mine in (first_lanes, jnp.logical_not(first_lanes)):
                stats += thirds(jnp.where(mine, stat, 0.0))
        stats = jnp.concatenate(stats + [jnp.zeros((4, 256), F32)], axis=0).astype(BF16)
        wides.append(nn(jnp.concatenate([hi, lo, stats], axis=0), e1[p]))
    for p in PAIRS:
        wide = wides[p]
        o1[p] = wide[0:128] + wide[128:256]
        for j in range(2):
            n = 2 * p + j
            l1s[n : n + 1] = jnp.sum(wide[256 + 3 * j : 259 + 3 * j], axis=0, keepdims=True)
            m1s[n : n + 1] = jnp.sum(wide[262 + 3 * j : 265 + 3 * j], axis=0, keepdims=True)

    copy(x2.at[1 - core], x2.at[1 - core], 5, to_mate).wait_recv()
    own_head = iota((48, 384), 0) // 8 == iota((48, 384), 1) // HD
    xs = x2[...].reshape(1024, 384)
    scores2 = nt(q2[...], xs)
    scores2 = jnp.where(lax.rem(iota((1, 1024), 1), 16) < 8, scores2, -1e30)
    top2 = jnp.max(scores2, axis=1, keepdims=True)
    weights2 = jnp.exp2((scores2 - top2) * SCALE).astype(BF16).astype(F32)
    p2[...] = weights2
    o2[...] = jnp.where(own_head, nn(pltpu.roll(weights2, 8, 1).astype(BF16), xs), 0.0)
    sum2 = jnp.sum(weights2, axis=1, keepdims=True)

    def expand2(part, hit2):
        hi, lo = halves(part)
        return tn(jnp.concatenate([hi, lo], axis=0), jnp.concatenate([hit2, hit2], axis=0))

    def expand2_right(part, hit2):
        hi, lo = halves(part)
        return tn(jnp.concatenate([hit2, hit2], axis=0), jnp.concatenate([hi, lo], axis=0))

    lane48 = iota((48, 48), 1)
    same_head = iota((48, 48), 0) // 8 == lax.rem(lane48, 8)
    table = jnp.zeros((48, 48), F32)
    for t, piece in enumerate(thirds(top2) + thirds(sum2)):
        table = jnp.where(lane48 // 8 == t, piece, table)
    table = jnp.where(same_head, table, 0.0).astype(BF16)
    stats2 = tn(table, e2[...])
    m2 = stats2[0:8] + stats2[8:16] + stats2[16:24]
    l2 = stats2[24:32] + stats2[32:40] + stats2[40:48]
    m0, l0, l1 = m0s[...], l0s[...], l1s[...]
    m1 = jnp.where(lax.rem(lane512, 4) == f1, m1s[...], -1e30)
    m2 = jnp.where(lax.rem(lane512, 64) == f2, m2, -1e30)
    highest = jnp.maximum(m0, jnp.maximum(m1, m2))
    c0 = jnp.exp2((m0 - highest) * SCALE)
    c1 = jnp.exp2((m1 - highest) * SCALE)
    c2 = jnp.exp2((m2 - highest) * SCALE)
    over = 1.0 / (c0 * l0 + c1 * l1 + c2 * l2)
    g0, g1, g2 = c0 * over, c1 * over, c2 * over
    gs[0] = g0
    gs[1] = g1
    gs[2] = g2
    fars = [expand2(o2[p * 16 : p * 16 + 16, cols(p)], e2[p * 16 : p * 16 + 16]) for p in PAIRS]
    for p in PAIRS:
        found = []
        for j in range(2):
            n = 2 * p + j
            part = slice(HD * j, HD * (j + 1))
            found.append(
                g0[n : n + 1] * o0[p, part] + g1[n : n + 1] * o1[p, part] + g2[n : n + 1] * fars[p][part]
            )
        both = jnp.concatenate(found, axis=0)
        at[p * 128 : p * 128 + 128, :] = both.astype(BF16)
        an[:, cols(p)] = both.T.astype(BF16)

    loads[3].wait()
    loads[4].wait()
    own_cols = pl.ds(pl.multiple_of(h * 384, 128), 384)
    other_cols = pl.ds(pl.multiple_of((1 - h) * 384, 128), 384)
    mxs[...] = nn(an[...], w_ref[:, other_cols]).astype(BF16)
    send_m = copy(mxs, mxr, 6, to_half)
    send_m.start()

    mate_rows = pl.ds(pl.multiple_of((1 - core) * 192, 64), 192)
    own_rows = pl.ds(pl.multiple_of(core * 192, 64), 192)
    wps[pl.ds(h * 12, 12)] = nn(at[mate_rows, :], g_ref[...]).astype(BF16).reshape(12, 16, 384)
    wpo[pl.ds(h * 12, 12)] = nn(at[own_rows, :], g_ref[...]).reshape(12, 16, 384)
    early_w = wps.at[pl.ds(h * 12, 12)]
    copy(early_w, wmr.at[pl.ds(h * 12, 12)], 7, to_mate).start()
    copy(goth, goth, 0, to_half).wait_recv()
    wps[pl.ds((1 - h) * 12, 12)] = nn(at[mate_rows, :], goth[...]).astype(BF16).reshape(12, 16, 384)
    send_w = copy(wps, wmr, 7, to_mate)
    late_w = wps.at[pl.ds((1 - h) * 12, 12)]
    copy(late_w, wmr.at[pl.ds((1 - h) * 12, 12)], 7, to_mate).start()
    gt[...] = (nt(w_ref[:, own_cols], g_ref[...]) + nt(w_ref[:, other_cols], goth[...])).astype(BF16)
    wpo[pl.ds((1 - h) * 12, 12)] = nn(at[own_rows, :], goth[...]).reshape(12, 16, 384)

    for n in range(6):
        own = slice(HD * n, HD * (n + 1))
        ds[n : n + 1] = jnp.sum(
            gt[own, :].astype(F32) * at[own, :].astype(F32), axis=0, keepdims=True
        )
    gs[...] = 0.125 * gs[...]

    def weighted(level, p):
        return jnp.concatenate(
            [
                (gt[HD * n : HD * (n + 1), :].astype(F32) * gs[level, n : n + 1]).astype(BF16)
                for n in (2 * p, 2 * p + 1)
            ],
            axis=0,
        )

    shares2 = gs[2] * ds[...]
    deltas2 = []
    for p in PAIRS:
        sixteen = slice(p * 16, p * 16 + 16)
        do2[sixteen, cols(p)] = jnp.where(pair16, nt(e2[sixteen], weighted(2, p)), 0.0).astype(BF16)
        share = jnp.where(row16 < 8, shares2[2 * p : 2 * p + 1], shares2[2 * p + 1 : 2 * p + 2])
        deltas2.append(jnp.sum(e2[sixteen].astype(F32) * share, axis=1, keepdims=True))
    delta2 = jnp.concatenate(deltas2, axis=0)

    xs = x2[...].reshape(1024, 384)
    weights2 = p2[...]
    grad_prob2 = pltpu.roll(nt(do2[...], xs), 1024 - 8, 1)
    dscore2 = weights2 * (grad_prob2 - delta2)
    left_side = jnp.concatenate([dscore2, 8.0 * pltpu.roll(weights2, 8, 1)], axis=0).astype(BF16)
    dx[...] = tn(left_side, jnp.concatenate([q2[...], do2[...]], axis=0)).reshape(2, CHIPS, 16, 384)
    dxs[...] = dx[1 - core].astype(BF16)
    send_x = copy(dxs, dxm, 11, to_mate)
    send_x.start()
    dq2[...] = jnp.where(own_head, nn(dscore2.astype(BF16), xs), 0.0)

    copy(wmr, wmr, 7, to_mate).wait_recv()
    wrs[...] = (wpo[...] + wmr[...].astype(F32)).astype(BF16)

    for i, device in enumerate(in_column):
        copy(wrs.at[pl.ds(other_rows[i] * OWNERS, OWNERS)], wyr.at[row], 8, device).start()

    fews = []
    for p in PAIRS:
        share = gs[1] * ds[...]
        stats = jnp.concatenate(
            thirds(share[2 * p : 2 * p + 1]) + thirds(share[2 * p + 1 : 2 * p + 2])
            + [jnp.zeros((10, TOK), F32)],
            axis=0,
        ).astype(BF16)
        fews.append(nt(jnp.concatenate([weighted(1, p), stats], axis=0), e1[p]))
    grads = [jnp.where(diagonal, fews[p][0:128], 0.0).astype(BF16) for p in PAIRS]
    deltas = [
        jnp.where(
            first_lanes,
            jnp.sum(fews[p][128:131], axis=0, keepdims=True),
            jnp.sum(fews[p][131:134], axis=0, keepdims=True),
        )
        for p in PAIRS
    ]
    values = [kv1[:, p, 128:256, :].reshape(TOK, 128) for p in PAIRS]
    grad_probs = [nn(values[p], grads[p]) for p in PAIRS]
    dscores = [(p1[p].astype(F32) * (grad_probs[p] - deltas[p])).astype(BF16) for p in PAIRS]
    for p in PAIRS:
        dk1[:, p, 0:128, :] = nt(dscores[p], q1t[p]).reshape(4, 128, 128)
        dk1[:, p, 128:256, :] = (8.0 * nt(p1[p], grads[p])).reshape(4, 128, 128)
    dks[0] = dk1[r_mate].astype(BF16)
    dks[1] = dk1[r_other].astype(BF16)
    send_k = copy(dks, dkm, 13, to_mate)

    copy(dxm, dxm, 11, to_mate).wait_recv()
    dxb[...] = (dx[core] + dxm[...].astype(F32)).astype(BF16)

    for i, device in enumerate(in_column):
        copy(dxb.at[pl.ds(other_rows[i] * PLANE, PLANE)], xyr.at[row], 12, device).start()

    send_k.start()
    wyr[row] = wrs[pl.ds(row * OWNERS, OWNERS)]
    copy(wyr.at[pl.ds(0, 3)], wyr.at[pl.ds(0, 3)], 8, to_mate).wait_recv()
    wy[...] = jnp.sum(wyr[...].astype(F32), axis=0).astype(BF16)
    for k in range(OWNERS):

        @pl.when(place != k)
        def _():
            copy(wy.at[k], wxr.at[place], 18, peer(row * PLANE + k)).start()

    firsts = [nn(k1t[p], dscores[p]) for p in PAIRS]
    for p in PAIRS:
        hi, lo = halves(jnp.where(diagonal, firsts[p], 0.0))
        wide = nn(jnp.concatenate([hi, lo], axis=0), e1[p])
        dqx[p] = wide[0:128] + wide[128:256] + expand2(
            dq2[p * 16 : p * 16 + 16, cols(p)], e2[p * 16 : p * 16 + 16]
        )
    nears = []

    def near_back(p):
        k_t, q_t, v = kt[p], qt[p], v_ref[:, cols(p)]
        grad_k = jnp.zeros((TOK, 128), F32)
        grad_v = jnp.zeros((TOK, 128), F32)
        grad_q = []
        grad = weighted(0, p)
        share = gs[0] * ds[...]
        for j in range(2):
            n = 2 * p + j
            grad_m = masked(grad, j)
            prob = p0[n]
            dscore = (prob.astype(F32) * (nn(v, grad_m) - share[n : n + 1])).astype(BF16)
            grad_q.append(nn(k_t[HD * j : HD * (j + 1)], dscore))
            grad_k = grad_k + nt(dscore, masked(q_t, j))
            grad_v = grad_v + nt(prob, grad_m)
        dq_ref[:, cols(p)] = (jnp.concatenate(grad_q, axis=0) + dqx[p]).T.astype(BF16)
        nears.append((grad_k, 8.0 * grad_v))

    near_back(0)
    copy(dkm, dkm, 13, to_mate).wait_recv()
    dkc[...] = (dk1[r_facing] + dkm[1].astype(F32)).astype(BF16)
    send_f = copy(dkc, dkr, 14, to_facing)
    send_f.start()
    @pl.when(owner)
    def _():
        wxr[place] = wy[place]
        copy(wxr.at[pl.ds(0, 7)], wxr.at[pl.ds(0, 7)], 18, to_mate).wait_recv()
        result = wfull.at[core, row * OWNERS + place]
        result[...] = jnp.sum(wxr[...].astype(F32), axis=0).astype(BF16)
        for device in in_plane:
            copy(result, result, 9, device).start()

    near_back(1)

    xyr[row] = dxb[own_row]
    copy(xyr.at[pl.ds(0, 3)], xyr.at[pl.ds(0, 3)], 12, to_mate).wait_recv()
    xb[...] = jnp.sum(xyr[...].astype(F32), axis=0).astype(BF16)
    for i, device in enumerate(in_plane):
        copy(xb.at[lax.rem(place + 1 + i, PLANE)], xr.at[place], 19, device).start()

    def plane_done(n_blocks):
        some = wfull.at[core, pl.ds(0, n_blocks)]
        copy(some, some, 9, to_mate).wait_recv()
        copy(wy.at[pl.ds(0, n_blocks)], wy.at[pl.ds(0, n_blocks)], 18, to_mate).wait_send()

    @pl.when(owner)
    def _():
        plane_done(OWNERS - 1)

    @pl.when(jnp.logical_not(owner))
    def _():
        plane_done(OWNERS)

    own_w = wfull.at[core, pl.ds(row * OWNERS, OWNERS)]
    for i, device in enumerate(in_column):
        copy(own_w, own_w, 20 + i, device).start()
    copy(own_w, own_w, 10, to_mate).start()
    near_back(2)

    outputs = [
        pltpu.make_async_copy(src, dst, osem.at[i])
        for i, (src, dst) in enumerate(
            (
                (mixed_ref, mixed_hbm), (dq_ref, dq_hbm), (dk_ref, dk_hbm),
                (dv_ref, dv_hbm), (dw_ref, dw_hbm),
            )
        )
    ]
    outputs[1].start()

    own_part = nn(an[...], w_ref[:, own_cols])
    copy(mxr, mxr, 6, to_half).wait_recv()
    mixed_ref[...] = (own_part + mxr[...].astype(F32)).astype(BF16)
    outputs[0].start()

    xr[place] = xb[place]
    copy(xr.at[pl.ds(0, 7)], xr.at[pl.ds(0, 7)], 19, to_mate).wait_recv()
    far = jnp.sum(xr[...].astype(F32), axis=0)
    copy(dkr, dkr, 14, to_facing).wait_recv()
    for p in PAIRS:
        near1 = dk1[r, p] + dkm[0, p].astype(F32) + dkr[p].astype(F32)
        near1 = jnp.concatenate([near1[0:128], near1[128:256]], axis=1)
        near1 = jnp.concatenate([jnp.where(left, near1, 0.0), jnp.where(left, 0.0, near1)], axis=0)
        hi, lo = halves(near1)
        few = jnp.concatenate([far[0:8, cols(p)], far[8:16, cols(p)]], axis=1)
        few = jnp.concatenate([jnp.where(left, few, 0.0), jnp.where(left, 0.0, few)], axis=0)
        total = tn(e1[p], hi) + tn(e1[p], lo) + expand2_right(few, e2[p * 16 : p * 16 + 16])
        dk_ref[:, cols(p)] = (nears[p][0] + total[:, 0:128]).astype(BF16)
        dv_ref[:, cols(p)] = (nears[p][1] + total[:, 128:256]).astype(BF16)
    outputs[2].start()
    outputs[3].start()

    for i in range(3):
        source = lax.rem(row + ROWS - 1 - i, ROWS)
        arrived = wfull.at[core, pl.ds(source * OWNERS, OWNERS)]
        copy(arrived, arrived, 20 + i, to_mate).wait_recv()
        copy(arrived, arrived, 10, to_mate).start()

    def write_w(half):
        for side_cols in range(2):
            dw_ref[pl.ds(pl.multiple_of(half * 192, 64), 192), side_cols * 384 : side_cols * 384 + 384] = wfull[
                half, side_cols * 12 : side_cols * 12 + 12
            ].reshape(192, 384)

    write_w(core)
    copy(wfull.at[1 - core], wfull.at[1 - core], 10, to_mate).wait_recv()
    write_w(1 - core)
    outputs[4].start()

    for sent in (send_g, send_a, send_b, send_c, send_m, send_w, send_x, send_k, send_f):
        sent.wait_send()
    copy(seven, seven, 4, to_mate).wait_send()
    copy(x2.at[core], x2.at[core], 5, to_mate).wait_send()
    for i in range(3):
        copy(own_blocks, own_blocks, 15 + i, to_mate).wait_send()
        copy(own_w, own_w, 20 + i, to_mate).wait_send()
    copy(wyr.at[pl.ds(0, 3)], wyr.at[pl.ds(0, 3)], 8, to_mate).wait_send()
    copy(xyr.at[pl.ds(0, 3)], xyr.at[pl.ds(0, 3)], 12, to_mate).wait_send()
    copy(xr.at[pl.ds(0, 7)], xr.at[pl.ds(0, 7)], 19, to_mate).wait_send()
    copy(wfull.at[core], wfull.at[core], 10, to_mate).wait_send()

    @pl.when(owner)
    def _():
        copy(wxr.at[pl.ds(0, 7)], wxr.at[pl.ds(0, 7)], 9, to_mate).wait_send()

    for output in outputs:
        output.wait()


def deliver(*refs):
    sources, targets, buffers, wide = refs[0:5], refs[5:10], refs[10:15], refs[15]
    in_sems, out_sems = refs[16:18]
    parts = [(i, half) for i in range(5) for half in range(2)]

    def rows(i, half):
        count = sources[i].shape[0] // 2
        return pl.ds(half * count, count)

    ins = [
        pltpu.make_async_copy(sources[i].at[rows(i, k)], buffers[i].at[rows(i, k)], in_sems.at[i, k])
        for i, k in parts
    ]
    for one in ins:
        one.start()
    outs = []
    for (i, k), one in zip(parts, ins):
        one.wait()
        source = buffers[i]
        if i == 4:
            wide[rows(i, k), :] = source[rows(i, k), :].astype(F32)
            source = wide
        outs.append(
            pltpu.make_async_copy(source.at[rows(i, k)], targets[i].at[rows(i, k)], out_sems.at[i, k])
        )
        outs[-1].start()
    for one in outs:
        one.wait()


def per_device(queries, keys, values, offsets, w_out, grad_mixed):
    anywhere = pl.BlockSpec(memory_space=pl.ANY)
    V = pltpu.VMEM
    block = jax.ShapeDtypeStruct((TOK, 384), BF16)
    scratch = [V((TOK, 384), BF16)] * 3 + [V((384, 768), BF16)] + [V((TOK, 384), BF16)] * 5 + [
        V((384, 768), BF16),
        V((4, 3, 256, 128), BF16),
        V((2, CHIPS, 16, 384), BF16),
        V((TOK, 384), BF16),
        V((3, 128, TOK), BF16),
        V((3, 128, TOK), BF16),
        V((3, 128, TOK), BF16),
        V((3, 128, TOK), BF16),
        V((3, 128, 256), BF16),
        V((48, 384), BF16),
        V((3, 256, TOK), BF16),
        V((48, TOK), BF16),
        V((6, TOK, TOK), BF16),
        V((3, TOK, 256), BF16),
        V((48, 1024), F32),
        V((3, 128, TOK), F32),
        V((3, 128, TOK), F32),
        V((48, 384), F32),
        V((8, TOK), F32),
        V((8, TOK), F32),
        V((8, TOK), F32),
        V((8, TOK), F32),
        V((3, 8, TOK), F32),
        V((8, TOK), F32),
        V((384, TOK), BF16),
        V((TOK, 384), BF16),
        V((384, TOK), BF16),
        V((TOK, 384), BF16),
        V((TOK, 384), BF16),
        V((24, 16, 384), BF16),
        V((24, 16, 384), F32),
        V((24, 16, 384), BF16),
        V((24, 16, 384), BF16),
        V((ROWS, OWNERS, 16, 384), BF16),
        V((OWNERS, 16, 384), BF16),
        V((PLANE, 16, 384), BF16),
        V((2, 24, 16, 384), BF16),
        V((48, 384), BF16),
        V((2, CHIPS, 16, 384), F32),
        V((CHIPS, 16, 384), BF16),
        V((CHIPS, 16, 384), BF16),
        V((CHIPS, 16, 384), BF16),
        V((ROWS, PLANE, 16, 384), BF16),
        V((PLANE, 16, 384), BF16),
        V((PLANE, 16, 384), BF16),
        V((48, 384), F32),
        V((3, 128, TOK), F32),
        V((4, 3, 256, 128), F32),
        V((2, 3, 256, 128), BF16),
        V((2, 3, 256, 128), BF16),
        V((3, 256, 128), BF16),
        V((3, 256, 128), BF16),
        pltpu.SemaphoreType.DMA((23,)),
        pltpu.SemaphoreType.DMA((23,)),
        pltpu.SemaphoreType.DMA((5,)),
        pltpu.SemaphoreType.DMA((5,)),
    ]
    results = pl.pallas_call(
        kernel,
        out_shape=(block, block, block, block, jax.ShapeDtypeStruct((384, 768), BF16)),
        in_specs=[pl.BlockSpec(memory_space=pltpu.SMEM)] + [anywhere] * 5,
        out_specs=(anywhere,) * 5,
        scratch_shapes=scratch,
        compiler_params=pltpu.CompilerParams(
            collective_id=0, has_side_effects=True, vmem_limit_bytes=60 << 20
        ),
    )(offsets, queries, keys, values, w_out, grad_mixed)
    return pl.pallas_call(
        deliver,
        out_shape=(block, block, block, block, jax.ShapeDtypeStruct((384, 768), F32)),
        in_specs=[anywhere] * 5,
        out_specs=(anywhere,) * 5,
        scratch_shapes=[V((TOK, 384), BF16)] * 4 + [
            V((384, 768), BF16),
            V((384, 768), F32),
            pltpu.SemaphoreType.DMA((5, 2)),
            pltpu.SemaphoreType.DMA((5, 2)),
        ],
        compiler_params=pltpu.CompilerParams(vmem_limit_bytes=60 << 20),
    )(*results)


def solution(mesh):
    in_specs = (
        P("seq", "head"),
        P("seq", "head"),
        P("seq", "head"),
        P(),
        P("head", None),
        P("seq", "head"),
    )
    out_specs = (
        P("seq", "head"),
        P("seq", "head"),
        P("seq", "head"),
        P("seq", "head"),
        P("head", None),
    )
    return jax.shard_map(
        per_device, mesh=mesh, in_specs=in_specs, out_specs=out_specs, check_vma=False
    )
```
